128 devices in a mesh: rows: 8 (over y, z_lo), cols: 16 (over x, z_hi, core).
Axes of the slice: x: 4, y: 4, z: 4 (z_hi: 2, z_lo: 2; z = z_hi * 2 + z_lo), core: 2. Of those that a mesh axis runs over, the one named last changes fastest.
Arguments:
- coarse: bfloat16 [16, 32, 128, 512], P('cols', 'rows'), may hold values from -35 to 35
- broad_entry_scale: float32 [512], replicated, may hold values from 0.1 to 1.9
- broad_entry_bias: float32 [512], replicated, may hold values from -2.5 to 2.5
- broad_entry_kernel: bfloat16 [3, 3, 512, 256], replicated, may hold values from -0.09375 to 0.09375
- broad_inner_scale: float32 [256], replicated, may hold values from 0.1 to 1.9
- broad_inner_bias: float32 [256], replicated, may hold values from -2.5 to 2.5
- broad_inner_kernel: bfloat16 [3, 3, 256, 256], replicated, may hold values from -0.125 to 0.125
- broad_skip_projection: bfloat16 [512, 256], replicated, may hold values from -0.25 to 0.25
- detail_entry_scale: float32 [256], replicated, may hold values from 0.1 to 1.9
- detail_entry_bias: float32 [256], replicated, may hold values from -2.5 to 2.5
- detail_entry_kernel: bfloat16 [3, 3, 256, 128], replicated, may hold values from -0.125 to 0.125
- detail_inner_scale: float32 [128], replicated, may hold values from 0.1 to 1.9
- detail_inner_bias: float32 [128], replicated, may hold values from -2.5 to 2.5
- detail_inner_kernel: bfloat16 [3, 3, 128, 128], replicated, may hold values from -0.1875 to 0.1875
- detail_skip_projection: bfloat16 [256, 128], replicated, may hold values from -0.375 to 0.375
Outputs:
- decoded: bfloat16 [16, 128, 512, 128], P(None, 'rows', 'cols')
The draws below stay inside these ranges and needn't reach their ends.
All inputs are finite; a program needn't handle non-finite values.
Results may differ from the reference program's by a relative error of at most 0.007.
Values may be sent and summed in bfloat16 or wider, within the bound.
No kernel may reach another device: no remote copies, remote signals or barrier semaphores. Data moves between devices by JAX's collectives and lax.ppermute only.
A program may use at most 64 MiB of HBM per device.

```python
import math
import jax
import jax.numpy as jnp
from jax import lax

C0 = 512
CA = 256
CB = 128
GROUPS = 32
CH = 4
CW = 8
IMAGES = 16
H0 = 32
W0 = 128


def draw_coarse(key, part):
    key = jax.random.fold_in(key, 7)
    key_values, key_channel, key_scale, key_offset = jax.random.split(key, 4)
    row_pos = jnp.arange(H0, dtype=jnp.float32) / H0
    col_pos = jnp.arange(W0, dtype=jnp.float32) / W0
    envelope = 3.0 ** (row_pos[None, :, None, None] + col_pos[None, None, :, None])
    shape = (IMAGES, H0, W0, C0)
    values = jnp.clip(jax.random.normal(key_values, shape, jnp.float32), -4.0, 4.0)
    channel = jnp.exp(jax.random.uniform(key_channel, (C0,), jnp.float32, math.log(0.3), math.log(3.0)))
    region_shape = (IMAGES, H0 // CH, W0 // CW, 1)
    region_scale = jax.random.uniform(key_scale, region_shape, jnp.float32, 0.35, 1.0)
    region_offset = jax.random.uniform(key_offset, region_shape, jnp.float32, -3.0, 3.0)
    region_scale = jnp.repeat(jnp.repeat(region_scale, CH, axis=1), CW, axis=2)
    region_offset = jnp.repeat(jnp.repeat(region_offset, CH, axis=1), CW, axis=2)
    return (values * envelope * channel * region_scale / 4.0 + region_offset).astype(jnp.bfloat16)


def centred(rng, extent, scale, bound, kind=jnp.bfloat16):
    result = jax.random.normal(rng, extent, jnp.float32) * scale
    return jnp.minimum(jnp.maximum(result, -bound), bound).astype(kind)


def setup_inputs(seed: int = 0) -> dict:
    key_of = jax.random.split(jax.random.key(seed), 16)
    return {
        "coarse": draw_coarse(jax.random.fold_in(key_of[15], 71), 0),
        "broad_entry_scale": jnp.clip(1.0 + 0.18 * jax.random.normal(key_of[1], (C0,), jnp.float32), 0.1, 1.9),
        "broad_entry_bias": centred(key_of[2], (C0,), 0.5, 2.5, jnp.float32),
        "broad_entry_kernel": centred(key_of[3], (3, 3, C0, CA), (9 * C0) ** -0.5, 0.09375),
        "broad_inner_scale": jnp.clip(1.0 + 0.18 * jax.random.normal(key_of[4], (CA,), jnp.float32), 0.1, 1.9),
        "broad_inner_bias": centred(key_of[5], (CA,), 0.5, 2.5, jnp.float32),
        "broad_inner_kernel": centred(key_of[6], (3, 3, CA, CA), (9 * CA) ** -0.5, 0.125),
        "broad_skip_projection": centred(key_of[7], (C0, CA), C0 ** -0.5, 0.25),
        "detail_entry_scale": jnp.clip(1.0 + 0.18 * jax.random.normal(key_of[8], (CA,), jnp.float32), 0.1, 1.9),
        "detail_entry_bias": centred(key_of[9], (CA,), 0.5, 2.5, jnp.float32),
        "detail_entry_kernel": centred(key_of[10], (3, 3, CA, CB), (9 * CA) ** -0.5, 0.125),
        "detail_inner_scale": jnp.clip(1.0 + 0.18 * jax.random.normal(key_of[11], (CB,), jnp.float32), 0.1, 1.9),
        "detail_inner_bias": centred(key_of[12], (CB,), 0.5, 2.5, jnp.float32),
        "detail_inner_kernel": centred(key_of[13], (3, 3, CB, CB), (9 * CB) ** -0.5, 0.1875),
        "detail_skip_projection": centred(key_of[14], (CA, CB), CA ** -0.5, 0.375),
    }


EPSILON = 1e-06

def enlarge_grid(value):
    return jnp.repeat(jnp.repeat(value, 2, axis=1), 2, axis=2)

def normalize(value, gain, shift):
    whole = value.astype(jnp.float32)
    count, height, width, chans = whole.shape
    grouped = whole.reshape(count, height, width, GROUPS, chans // GROUPS)
    center = lax.optimization_barrier(jnp.mean(grouped, axis=(1, 2, 4), keepdims=True))
    spread = lax.optimization_barrier(jnp.mean((grouped - center) ** 2, axis=(1, 2, 4), keepdims=True))
    scaled = ((grouped - center) * lax.rsqrt(spread + EPSILON)).reshape(count, height, width, chans)
    scaled = scaled * gain.astype(jnp.float32) + shift.astype(jnp.float32)
    return jax.nn.silu(scaled).astype(jnp.bfloat16)

def convolve(value, kernel):
    return lax.conv_general_dilated(value, kernel, (1, 1), 'SAME', dimension_numbers=('NHWC', 'HWIO', 'NHWC'), preferred_element_type=jnp.float32)

def residual_unit(input_pixels, entry_scale, entry_bias, entry_kernel, inner_scale, inner_bias, inner_kernel, skip_projection):
    middle = convolve(normalize(input_pixels, entry_scale, entry_bias), entry_kernel).astype(jnp.bfloat16)
    branch = convolve(normalize(middle, inner_scale, inner_bias), inner_kernel)
    count, height, width, chans = input_pixels.shape
    direct = jnp.dot(input_pixels.reshape(-1, chans), skip_projection, preferred_element_type=jnp.float32)
    return (direct.reshape(count, height, width, -1) + branch).astype(jnp.bfloat16)

def reference(coarse, broad_entry_scale, broad_entry_bias, broad_entry_kernel, broad_inner_scale, broad_inner_bias, broad_inner_kernel, broad_skip_projection, detail_entry_scale, detail_entry_bias, detail_entry_kernel, detail_inner_scale, detail_inner_bias, detail_inner_kernel, detail_skip_projection):
    broad_output = residual_unit(enlarge_grid(coarse), broad_entry_scale, broad_entry_bias, broad_entry_kernel, broad_inner_scale, broad_inner_bias, broad_inner_kernel, broad_skip_projection)
    return residual_unit(enlarge_grid(broad_output), detail_entry_scale, detail_entry_bias, detail_entry_kernel, detail_inner_scale, detail_inner_bias, detail_inner_kernel, detail_skip_projection)
```

```python
import functools

import jax
import jax.numpy as jnp
from jax import lax
from jax.experimental import pallas as pl
from jax.experimental.pallas import tpu as pltpu
from jax.sharding import PartitionSpec as P

GROUPS = 32
EPSILON = 1e-06
F32 = jnp.float32
BF16 = jnp.bfloat16
ROWS = 8
COLS = 16
W = 128
VMEM_LIMIT = 48 * 1024 * 1024


def call(kernel, out_shape, scratch=(), flops=0, name=None):
    return pl.pallas_call(
        kernel,
        out_shape=out_shape,
        scratch_shapes=list(scratch),
        name=name,
        cost_estimate=pl.CostEstimate(flops=flops, bytes_accessed=0, transcendentals=0),
        compiler_params=pltpu.CompilerParams(vmem_limit_bytes=VMEM_LIMIT),
    )


def group_sum(v, size):
    count = v.shape[-1]
    lane = lax.broadcasted_iota(jnp.int32, v.shape, 1)
    step = 1
    while step < size:
        before = pltpu.roll(v, step, 1)
        after = pltpu.roll(v, count - step, 1)
        v = v + jnp.where((lane & step) != 0, before, after)
        step *= 2
    return v


def moments(parts, held):
    both = jnp.concatenate([parts[d] for d in range(ROWS)], axis=0)
    chans = both.shape[1] // 2
    size = chans // GROUPS
    sums, squares = both[:, :chans], both[:, chans:]
    entries = float(ROWS * held * size)
    total = jnp.broadcast_to(jnp.sum(sums, axis=0, keepdims=True), sums.shape)
    mean = group_sum(total, size) / entries
    off = sums / float(held) - mean
    spread = jnp.sum(squares + float(held) * off * off, axis=0, keepdims=True)
    spread = group_sum(jnp.broadcast_to(spread, sums.shape), size) / entries
    return mean, lax.rsqrt(spread + EPSILON)


def tile_lanes(v, times):
    return jnp.concatenate([v] * times, axis=1) if times > 1 else v


def active(value, mean, gain, shift):
    y = (value.astype(F32) - mean) * gain + shift
    half = 0.5 * y
    return half + half * jnp.tanh(half)


def block_moments(blocks):
    n = blocks[0].shape[0]
    sums, squares = [], []
    for block in blocks:
        s = jnp.sum(block, axis=0, keepdims=True)
        d = block - s / float(n)
        sums.append(s)
        squares.append(jnp.sum(d * d, axis=0, keepdims=True))
    return merge_moments(sums, squares, n)


def merge_moments(sums, squares, n):
    total = functools.reduce(jnp.add, sums)
    mean = total / float(n * len(sums))
    out = functools.reduce(jnp.add, squares)
    for s in sums:
        off = s / float(n) - mean
        out = out + float(n) * off * off
    return jnp.concatenate([total, out], axis=1)


def publish(ref, vector):
    for d in range(ROWS):
        ref[d] = vector


def next_col(v):
    col = lax.broadcasted_iota(jnp.int32, v.shape, 0) % W
    return jnp.where(col == W - 1, 0.0, pltpu.roll(v, v.shape[0] - 1, 0))


def last_col(v):
    col = lax.broadcasted_iota(jnp.int32, v.shape, 0) % W
    return jnp.where(col == 0, 0.0, pltpu.roll(v, 1, 0))


def edge_flags():
    row = lax.axis_index("rows")
    return row == 0, row == ROWS - 1


def mm(a, b):
    return jnp.dot(a, b, preferred_element_type=F32)


def coarse_stats_kernel(x_ref, out_ref):
    x = x_ref[...].astype(F32).reshape(4 * W, 512)
    publish(out_ref, block_moments([x]))


def pack_broad_kernel(k_ref, out_ref):
    rows = (((0,), (1, 2)), ((0, 1), (2,)))
    step = 128
    for a in range(2):
        for t in range(2):
            for c in range(0, 512, step):
                col = [
                    functools.reduce(
                        jnp.add, [k_ref[ky, kx, c : c + step, :].astype(F32) for ky in rows[a][t]]
                    )
                    for kx in range(3)
                ]
                for n, v in enumerate((col[0], col[1] + col[2], col[0] + col[1], col[2])):
                    out_ref[a, t * 512 + c : t * 512 + c + step, n * 256 : (n + 1) * 256] = v.astype(BF16)


def pack_detail_kernel(k_ref, x_ref, z_ref):
    rows = (((0,), (1, 2)), ((0, 1), (2,)))
    for a in range(2):
        for t in range(2):
            col = [
                functools.reduce(jnp.add, [k_ref[ky, kx].astype(F32) for ky in rows[a][t]])
                for kx in range(3)
            ]
            x_ref[a, t] = jnp.concatenate([col[0] + col[1], col[0]], axis=1).astype(BF16)
            z_ref[a, t] = jnp.concatenate([col[2], col[1] + col[2]], axis=1).astype(BF16)


def pack_inner_kernel(k_ref, main_ref, side_ref):
    zero = jnp.zeros((128, 128), BF16)
    for ky in range(3):
        k = [k_ref[ky, kx] for kx in range(3)]
        table = (
            (zero, zero, k[2], k[1]),
            (k[1], k[0], zero, zero),
            (k[2], k[1], k[0], zero),
            (zero, k[2], k[1], k[0]),
        )
        for i, line in enumerate(table):
            for o, v in enumerate(line):
                main_ref[ky * 512 + i * 128 : ky * 512 + (i + 1) * 128, o * 128 : (o + 1) * 128] = v
        base = ky * 256
        side_ref[base : base + 128, 0:128] = k[0]
        side_ref[base : base + 128, 128:256] = zero
        side_ref[base + 128 : base + 256, 0:128] = zero
        side_ref[base + 128 : base + 256, 128:256] = k[2]


def broad_entry_kernel_body(x_ref, up_ref, down_ref, parts_ref, gain_ref, shift_ref, w_ref, out_ref, stat_ref, an):
    first, last = edge_flags()
    mean, rate = moments(parts_ref, 4 * W)
    mean, gain, shift = mean[:1], rate[:1] * gain_ref[...], shift_ref[...]
    keep_up = jnp.where(first, 0.0, 1.0)
    keep_down = jnp.where(last, 0.0, 1.0)
    for h in range(2):
        an[h] = (active(up_ref[h], mean, gain, shift) * keep_up).astype(BF16)
        an[6 + h] = (active(down_ref[h], mean, gain, shift) * keep_down).astype(BF16)
    for h in range(4):
        an[2 + h] = active(x_ref[h], mean, gain, shift).astype(BF16)
    blocks = []
    for a in range(2):
        near = an[a : a + 6].reshape(6 * W, 512)
        far = an[a + 1 : a + 7].reshape(6 * W, 512)
        both = jnp.concatenate([near, far], axis=1)
        for b in range(2):
            z = [mm(both, w_ref[a, :, n * 256 : (n + 1) * 256]) for n in (2 * b, 2 * b + 1)]
            v = last_col(z[0]) + z[1] if b == 0 else z[0] + next_col(z[1])
            v = v.astype(BF16)
            for h in range(6):
                out_ref[2 * h + a, :, b * 256 : (b + 1) * 256] = v[h * W : (h + 1) * W]
            blocks.append(v[W : 5 * W].astype(F32))
    publish(stat_ref, block_moments(blocks))


def broad_inner_kernel_body(
    h_ref, x_ref, up_ref, down_ref, parts_ref, gain_ref, shift_ref, w_ref, p_ref, out_ref, stat_ref, an
):
    first, last = edge_flags()
    mean, rate = moments(parts_ref, 8 * 2 * W)
    mean, gain, shift = mean[:1], rate[:1] * gain_ref[...], shift_ref[...]
    mean, gain, shift = (tile_lanes(v, 2) for v in (mean, gain, shift))
    keep_up = jnp.where(first, 0.0, 1.0)
    keep_down = jnp.where(last, 0.0, 1.0)
    for i in range(12):
        v = active(h_ref[i], mean, gain, shift)
        if i < 2:
            v = v * keep_up
        elif i >= 10:
            v = v * keep_down
        an[i] = v.astype(BF16)
    skip_in = jnp.concatenate([up_ref[1]] + [x_ref[h] for h in range(4)] + [down_ref[0]], axis=0)
    skip = mm(skip_in, p_ref[...])
    w = w_ref
    even_w = jnp.concatenate([w[ky * 768 + 256 : ky * 768 + 768] for ky in range(3)], axis=0)
    odd_w = jnp.concatenate([w[ky * 768 : ky * 768 + 512] for ky in range(3)], axis=0)
    even_side = jnp.concatenate([w[ky * 768 : ky * 768 + 256] for ky in range(3)], axis=0)
    odd_side = jnp.concatenate([w[ky * 768 + 512 : ky * 768 + 768] for ky in range(3)], axis=0)
    evens, odds = [], []
    count = 5
    for j in range(0, 10, count):
        main = jnp.concatenate([an[j + ky : j + ky + count].reshape(count * W, 512) for ky in range(3)], axis=1)
        even_in = jnp.concatenate(
            [an[j + ky : j + ky + count, :, 0:256].reshape(count * W, 256) for ky in range(3)], axis=1
        )
        odd_in = jnp.concatenate(
            [an[j + ky : j + ky + count, :, 256:512].reshape(count * W, 256) for ky in range(3)], axis=1
        )
        extra = jnp.concatenate([skip[(i + 1) // 2 * W : ((i + 1) // 2 + 1) * W] for i in range(j, j + count)], axis=0)
        even = (mm(main, even_w) + last_col(mm(odd_in, even_side)) + extra).astype(BF16)
        odd = (mm(main, odd_w) + next_col(mm(even_in, odd_side)) + extra).astype(BF16)
        for i in range(count):
            out_ref[j + i, :, 0:256] = even[i * W : (i + 1) * W]
            out_ref[j + i, :, 256:512] = odd[i * W : (i + 1) * W]
        lo, hi = (W, count * W) if j == 0 else (0, (count - 1) * W)
        evens.append(even[lo:hi].astype(F32))
        odds.append(odd[lo:hi].astype(F32))
    publish(stat_ref, block_moments(evens + odds))


def detail_entry_kernel_body(x_ref, parts_ref, gain_ref, shift_ref, wx_ref, wz_ref, out_ref, stat_ref, an):
    first, last = edge_flags()
    mean, rate = moments(parts_ref, 8 * 2 * W)
    mean, gain, shift = mean[:1], rate[:1] * gain_ref[...], shift_ref[...]
    mean, gain, shift = (tile_lanes(v, 2) for v in (mean, gain, shift))
    keep_up = jnp.where(first, 0.0, 1.0)
    keep_down = jnp.where(last, 0.0, 1.0)
    for i in range(10):
        v = active(x_ref[i], mean, gain, shift)
        if i < 1:
            v = v * keep_up
        elif i >= 9:
            v = v * keep_down
        an[i] = v.astype(BF16)
    blocks = []
    for a in range(2):
        lhs = [an[t : t + 9].reshape(9 * W, 512) for t in range(2)]
        main = jnp.concatenate(lhs, axis=1)
        odd = jnp.concatenate([v[:, 256:512] for v in lhs], axis=1)
        even = jnp.concatenate([v[:, 0:256] for v in lhs], axis=1)
        wx = [wx_ref[a, t] for t in range(2)]
        wz = [wz_ref[a, t] for t in range(2)]
        middle = mm(main, jnp.concatenate([wx[0], wz[0], wx[1], wz[1]], axis=0))
        right = mm(odd, jnp.concatenate(wx, axis=0))
        left = mm(even, jnp.concatenate(wz, axis=0))
        q3 = (right[:, 0:128] + next_col(left[:, 0:128])).astype(BF16)
        q0 = (last_col(right[:, 128:256]) + left[:, 128:256]).astype(BF16)
        middle = middle.astype(BF16)
        for i in range(9):
            f = 2 * i + 1 - a
            out_ref[f, :, 0:128] = q3[i * W : (i + 1) * W]
            out_ref[f, :, 128:256] = q0[i * W : (i + 1) * W]
            out_ref[f, :, 256:512] = middle[i * W : (i + 1) * W]
        lo, hi = (W, 9 * W) if a == 1 else (0, 8 * W)
        for v in (q3, q0, middle[:, 0:128], middle[:, 128:256]):
            blocks.append(v[lo:hi].astype(F32))
    publish(stat_ref, block_moments(blocks))


def detail_inner_kernel_body(
    h_ref, x_ref, parts_ref, gain_ref, shift_ref, w_ref, side_ref, p_ref, out_ref, an, tmp
):
    first, last = edge_flags()
    mean, rate = moments(parts_ref, 16 * 4 * W)
    mean, gain, shift = mean[:1], rate[:1] * gain_ref[...], shift_ref[...]
    mean, gain, shift = (tile_lanes(v, 4) for v in (mean, gain, shift))
    keep_up = jnp.where(first, 0.0, 1.0)
    keep_down = jnp.where(last, 0.0, 1.0)
    for i in range(18):
        v = active(h_ref[i], mean, gain, shift)
        if i < 1:
            v = v * keep_up
        elif i >= 17:
            v = v * keep_down
        an[i] = v.astype(BF16)
    count = 4
    for f in range(0, 16, count):
        rows = [an[f + ky : f + ky + count].reshape(count * W, 512) for ky in range(3)]
        main = mm(jnp.concatenate(rows, axis=1), w_ref[...])
        side = mm(jnp.concatenate([v[:, 0:256] for v in rows], axis=1), side_ref[...])
        raw = x_ref[1 + f // 2 : 1 + f // 2 + count // 2].reshape(count // 2 * W, 512)
        skips = [mm(raw[:, 0:256], p_ref[...]), mm(raw[:, 256:512], p_ref[...])]
        skips = [
            jnp.concatenate([s[i // 2 * W : (i // 2 + 1) * W] for i in range(count)], axis=0) for s in skips
        ]
        cols = [main[:, o * 128 : (o + 1) * 128] + skips[o // 2] for o in range(4)]
        cols[0] = cols[0] + last_col(side[:, 0:128])
        cols[3] = cols[3] + next_col(side[:, 128:256])
        for i in range(count):
            for o in range(4):
                tmp[i, pl.ds(o, W, stride=4), :] = cols[o][i * W : (i + 1) * W]
            out_ref[:, f + i] = tmp[i].reshape(COLS, 32, 128).astype(BF16)


def swap(parts):
    return lax.all_to_all(parts, "rows", 0, 0, tiled=True)


def shape(*dims, dtype=BF16):
    return jax.ShapeDtypeStruct(dims, dtype)


def line(v):
    return v.reshape(1, -1)


def body(
    coarse,
    broad_entry_scale,
    broad_entry_bias,
    broad_entry_kernel,
    broad_inner_scale,
    broad_inner_bias,
    broad_inner_kernel,
    broad_skip_projection,
    detail_entry_scale,
    detail_entry_bias,
    detail_entry_kernel,
    detail_inner_scale,
    detail_inner_bias,
    detail_inner_kernel,
    detail_skip_projection,
):
    x = coarse.reshape(4, W, 512)
    up = lax.ppermute(x[2:], "rows", [(i, i + 1) for i in range(ROWS - 1)])
    down = lax.ppermute(x[:2], "rows", [(i + 1, i) for i in range(ROWS - 1)])
    stat = lambda c: shape(ROWS, 1, 2 * c, dtype=F32)
    parts = swap(call(coarse_stats_kernel, stat(512), name="coarse_stats")(x))
    packed = call(pack_broad_kernel, shape(2, 1024, 1024), name="pack_broad", flops=1 << 24)(broad_entry_kernel)
    wide_h, parts = call(
        broad_entry_kernel_body,
        (shape(12, W, 512), stat(256)),
        [pltpu.VMEM((8, W, 512), BF16)],
        name="broad_entry",
        flops=1 << 32,
    )(x, up, down, parts, line(broad_entry_scale), line(broad_entry_bias), packed)
    parts = swap(parts)
    wide_out, parts = call(
        broad_inner_kernel_body,
        (shape(10, W, 512), stat(256)),
        [pltpu.VMEM((12, W, 512), BF16)],
        name="broad_inner",
        flops=1 << 32,
    )(
        wide_h,
        x,
        up,
        down,
        parts,
        line(broad_inner_scale),
        line(broad_inner_bias),
        broad_inner_kernel.reshape(9 * 256, 256),
        broad_skip_projection,
    )
    parts = swap(parts)
    wx, wz = call(
        pack_detail_kernel, (shape(2, 2, 256, 256), shape(2, 2, 256, 256)), name="pack_detail", flops=1 << 22
    )(detail_entry_kernel)
    fine_h, parts = call(
        detail_entry_kernel_body,
        (shape(18, W, 512), stat(128)),
        [pltpu.VMEM((10, W, 512), BF16)],
        name="detail_entry",
        flops=1 << 32,
    )(wide_out, parts, line(detail_entry_scale), line(detail_entry_bias), wx, wz)
    parts = swap(parts)
    main, side = call(
        pack_inner_kernel, (shape(1536, 512), shape(768, 256)), name="pack_inner", flops=1 << 22
    )(detail_inner_kernel)
    decoded = call(
        detail_inner_kernel_body,
        shape(COLS, 16, 32, 128),
        [pltpu.VMEM((18, W, 512), BF16), pltpu.VMEM((4, 4 * W, 128), F32)],
        name="detail_inner",
        flops=1 << 32,
    )(
        fine_h,
        wide_out,
        parts,
        line(detail_inner_scale),
        line(detail_inner_bias),
        main,
        side,
        detail_skip_projection,
    )
    return lax.all_to_all(decoded, "cols", 0, 0, tiled=True)


def solution(mesh):
    return jax.shard_map(
        body,
        mesh=mesh,
        in_specs=(P("cols", "rows", None, None),) + (P(),) * 14,
        out_specs=P(None, "rows", "cols", None),
        check_vma=False,
    )
```

```python
import functools

import jax
import jax.numpy as jnp
from jax import lax
from jax.experimental import pallas as pl
from jax.experimental.pallas import tpu as pltpu
from jax.sharding import PartitionSpec as P

GROUPS = 32
EPSILON = 1e-06
F32 = jnp.float32
BF16 = jnp.bfloat16
ROWS = 8
COLS = 16
W = 128
VMEM_LIMIT = 24 * 1024 * 1024


def call(kernel, out_shape, scratch=(), flops=0, name=None):
    return pl.pallas_call(
        kernel,
        out_shape=out_shape,
        scratch_shapes=list(scratch),
        name=name,
        cost_estimate=pl.CostEstimate(flops=flops, bytes_accessed=0, transcendentals=0),
        compiler_params=pltpu.CompilerParams(vmem_limit_bytes=VMEM_LIMIT),
    )


def group_sum(v, size):
    count = v.shape[-1]
    lane = lax.broadcasted_iota(jnp.int32, v.shape, 1)
    step = 1
    while step < size:
        before = pltpu.roll(v, step, 1)
        after = pltpu.roll(v, count - step, 1)
        v = v + jnp.where((lane & step) != 0, before, after)
        step *= 2
    return v


def moments(parts, held):
    both = jnp.concatenate([parts[d] for d in range(ROWS)], axis=0)
    chans = both.shape[1] // 2
    size = chans // GROUPS
    sums, squares = both[:, :chans], both[:, chans:]
    entries = float(ROWS * held * size)
    total = jnp.broadcast_to(jnp.sum(sums, axis=0, keepdims=True), sums.shape)
    mean = group_sum(total, size) / entries
    off = sums / float(held) - mean
    spread = jnp.sum(squares + float(held) * off * off, axis=0, keepdims=True)
    spread = group_sum(jnp.broadcast_to(spread, sums.shape), size) / entries
    return mean, lax.rsqrt(spread + EPSILON)


def tile_lanes(v, times):
    return jnp.concatenate([v] * times, axis=1) if times > 1 else v


def active(value, mean, gain, shift):
    y = (value.astype(F32) - mean) * gain + shift
    half = 0.5 * y
    return half + half * jnp.tanh(half)


def block_moments(blocks):
    n = blocks[0].shape[0]
    sums, squares = [], []
    for block in blocks:
        s = jnp.sum(block, axis=0, keepdims=True)
        d = block - s / float(n)
        sums.append(s)
        squares.append(jnp.sum(d * d, axis=0, keepdims=True))
    return merge_moments(sums, squares, n)


def merge_moments(sums, squares, n):
    total = functools.reduce(jnp.add, sums)
    mean = total / float(n * len(sums))
    out = functools.reduce(jnp.add, squares)
    for s in sums:
        off = s / float(n) - mean
        out = out + float(n) * off * off
    return jnp.concatenate([total, out], axis=1)


def publish(ref, vector):
    for d in range(ROWS):
        ref[d] = vector


def next_col(v):
    col = lax.broadcasted_iota(jnp.int32, v.shape, 0) % W
    return jnp.where(col == W - 1, 0.0, pltpu.roll(v, v.shape[0] - 1, 0))


def last_col(v):
    col = lax.broadcasted_iota(jnp.int32, v.shape, 0) % W
    return jnp.where(col == 0, 0.0, pltpu.roll(v, 1, 0))


def edge_flags():
    row = lax.axis_index("rows")
    return row == 0, row == ROWS - 1


def mm(a, b):
    return jnp.dot(a, b, preferred_element_type=F32)


def coarse_stats_kernel(x_ref, out_ref, head_ref, tail_ref):
    x = x_ref[...].astype(F32).reshape(4 * W, 512)
    head_ref[...] = x_ref[0:2]
    tail_ref[...] = x_ref[2:4]
    publish(out_ref, block_moments([x]))


def pack_broad(k_ref, out_ref):
    rows = (((0,), (1, 2)), ((0, 1), (2,)))
    step = 128
    for a in range(2):
        for t in range(2):
            for c in range(0, 512, step):
                col = [
                    functools.reduce(
                        jnp.add, [k_ref[ky, kx, c : c + step, :].astype(F32) for ky in rows[a][t]]
                    )
                    for kx in range(3)
                ]
                for n, v in enumerate((col[0], col[1] + col[2], col[0] + col[1], col[2])):
                    out_ref[a, t * 512 + c : t * 512 + c + step, n * 256 : (n + 1) * 256] = v.astype(BF16)


def pack_detail(k_ref, x_ref, z_ref):
    rows = (((0,), (1, 2)), ((0, 1), (2,)))
    for a in range(2):
        for t in range(2):
            col = [
                functools.reduce(jnp.add, [k_ref[ky, kx].astype(F32) for ky in rows[a][t]])
                for kx in range(3)
            ]
            x_ref[a, t] = jnp.concatenate([col[0] + col[1], col[0]], axis=1).astype(BF16)
            z_ref[a, t] = jnp.concatenate([col[2], col[1] + col[2]], axis=1).astype(BF16)


def pack_inner(k_ref, main_ref, side_ref):
    zero = jnp.zeros((128, 128), BF16)
    for ky in range(3):
        k = [k_ref[ky, kx] for kx in range(3)]
        table = (
            (zero, zero, k[2], k[1]),
            (k[1], k[0], zero, zero),
            (k[2], k[1], k[0], zero),
            (zero, k[2], k[1], k[0]),
        )
        for i, line in enumerate(table):
            for o, v in enumerate(line):
                main_ref[ky * 512 + i * 128 : ky * 512 + (i + 1) * 128, o * 128 : (o + 1) * 128] = v
        base = ky * 256
        side_ref[base : base + 128, 0:128] = k[0]
        side_ref[base : base + 128, 128:256] = zero
        side_ref[base + 128 : base + 256, 0:128] = zero
        side_ref[base + 128 : base + 256, 128:256] = k[2]


def broad_entry_kernel_body(x_ref, up_ref, down_ref, parts_ref, gain_ref, shift_ref, k_ref, out_ref, stat_ref, an, w_ref):
    pack_broad(k_ref, w_ref)
    first, last = edge_flags()
    mean, rate = moments(parts_ref, 4 * W)
    mean, gain, shift = mean[:1], rate[:1] * gain_ref[...], shift_ref[...]
    keep_up = jnp.where(first, 0.0, 1.0)
    keep_down = jnp.where(last, 0.0, 1.0)
    for h in range(2):
        an[h] = (active(up_ref[h], mean, gain, shift) * keep_up).astype(BF16)
        an[6 + h] = (active(down_ref[h], mean, gain, shift) * keep_down).astype(BF16)
    for h in range(4):
        an[2 + h] = active(x_ref[h], mean, gain, shift).astype(BF16)
    blocks = []
    for a in range(2):
        near = an[a : a + 6].reshape(6 * W, 512)
        far = an[a + 1 : a + 7].reshape(6 * W, 512)
        both = jnp.concatenate([near, far], axis=1)
        for b in range(2):
            z = [mm(both, w_ref[a, :, n * 256 : (n + 1) * 256]) for n in (2 * b, 2 * b + 1)]
            v = last_col(z[0]) + z[1] if b == 0 else z[0] + next_col(z[1])
            v = v.astype(BF16)
            for h in range(6):
                out_ref[2 * h + a, :, b * 256 : (b + 1) * 256] = v[h * W : (h + 1) * W]
            blocks.append(v[W : 5 * W].astype(F32))
    publish(stat_ref, block_moments(blocks))


def broad_inner_kernel_body(
    h_ref, x_ref, up_ref, down_ref, parts_ref, gain_ref, shift_ref, w_ref, p_ref, out_ref, stat_ref, an
):
    first, last = edge_flags()
    mean, rate = moments(parts_ref, 8 * 2 * W)
    mean, gain, shift = mean[:1], rate[:1] * gain_ref[...], shift_ref[...]
    mean, gain, shift = (tile_lanes(v, 2) for v in (mean, gain, shift))
    keep_up = jnp.where(first, 0.0, 1.0)
    keep_down = jnp.where(last, 0.0, 1.0)
    for i in range(12):
        v = active(h_ref[i], mean, gain, shift)
        if i < 2:
            v = v * keep_up
        elif i >= 10:
            v = v * keep_down
        an[i] = v.astype(BF16)
    skip_in = jnp.concatenate([up_ref[1]] + [x_ref[h] for h in range(4)] + [down_ref[0]], axis=0)
    skip = mm(skip_in, p_ref[...])
    w = w_ref
    even_w = jnp.concatenate([w[ky * 768 + 256 : ky * 768 + 768] for ky in range(3)], axis=0)
    odd_w = jnp.concatenate([w[ky * 768 : ky * 768 + 512] for ky in range(3)], axis=0)
    even_side = jnp.concatenate([w[ky * 768 : ky * 768 + 256] for ky in range(3)], axis=0)
    odd_side = jnp.concatenate([w[ky * 768 + 512 : ky * 768 + 768] for ky in range(3)], axis=0)
    evens, odds = [], []
    count = 5
    for j in range(0, 10, count):
        main = jnp.concatenate([an[j + ky : j + ky + count].reshape(count * W, 512) for ky in range(3)], axis=1)
        even_in = jnp.concatenate(
            [an[j + ky : j + ky + count, :, 0:256].reshape(count * W, 256) for ky in range(3)], axis=1
        )
        odd_in = jnp.concatenate(
            [an[j + ky : j + ky + count, :, 256:512].reshape(count * W, 256) for ky in range(3)], axis=1
        )
        extra = jnp.concatenate([skip[(i + 1) // 2 * W : ((i + 1) // 2 + 1) * W] for i in range(j, j + count)], axis=0)
        even = (mm(main, even_w) + last_col(mm(odd_in, even_side)) + extra).astype(BF16)
        odd = (mm(main, odd_w) + next_col(mm(even_in, odd_side)) + extra).astype(BF16)
        for i in range(count):
            out_ref[j + i, :, 0:256] = even[i * W : (i + 1) * W]
            out_ref[j + i, :, 256:512] = odd[i * W : (i + 1) * W]
        lo, hi = (W, count * W) if j == 0 else (0, (count - 1) * W)
        evens.append(even[lo:hi].astype(F32))
        odds.append(odd[lo:hi].astype(F32))
    publish(stat_ref, block_moments(evens + odds))


def detail_entry_kernel_body(x_ref, parts_ref, gain_ref, shift_ref, k_ref, out_ref, stat_ref, an, wx_ref, wz_ref):
    pack_detail(k_ref, wx_ref, wz_ref)
    first, last = edge_flags()
    mean, rate = moments(parts_ref, 8 * 2 * W)
    mean, gain, shift = mean[:1], rate[:1] * gain_ref[...], shift_ref[...]
    mean, gain, shift = (tile_lanes(v, 2) for v in (mean, gain, shift))
    keep_up = jnp.where(first, 0.0, 1.0)
    keep_down = jnp.where(last, 0.0, 1.0)
    for i in range(10):
        v = active(x_ref[i], mean, gain, shift)
        if i < 1:
            v = v * keep_up
        elif i >= 9:
            v = v * keep_down
        an[i] = v.astype(BF16)
    blocks = []
    for a in range(2):
        lhs = [an[t : t + 9].reshape(9 * W, 512) for t in range(2)]
        main = jnp.concatenate(lhs, axis=1)
        odd = jnp.concatenate([v[:, 256:512] for v in lhs], axis=1)
        even = jnp.concatenate([v[:, 0:256] for v in lhs], axis=1)
        wx = [wx_ref[a, t] for t in range(2)]
        wz = [wz_ref[a, t] for t in range(2)]
        middle = mm(main, jnp.concatenate([wx[0], wz[0], wx[1], wz[1]], axis=0))
        right = mm(odd, jnp.concatenate(wx, axis=0))
        left = mm(even, jnp.concatenate(wz, axis=0))
        q3 = (right[:, 0:128] + next_col(left[:, 0:128])).astype(BF16)
        q0 = (last_col(right[:, 128:256]) + left[:, 128:256]).astype(BF16)
        middle = middle.astype(BF16)
        for i in range(9):
            f = 2 * i + 1 - a
            out_ref[f, :, 0:128] = q3[i * W : (i + 1) * W]
            out_ref[f, :, 128:256] = q0[i * W : (i + 1) * W]
            out_ref[f, :, 256:512] = middle[i * W : (i + 1) * W]
        lo, hi = (W, 9 * W) if a == 1 else (0, 8 * W)
        for v in (q3, q0, middle[:, 0:128], middle[:, 128:256]):
            blocks.append(v[lo:hi].astype(F32))
    publish(stat_ref, block_moments(blocks))


def detail_inner_kernel_body(
    h_ref, x_ref, parts_ref, gain_ref, shift_ref, k_ref, p_ref, out_ref, an, tmp, w_ref, side_ref
):
    pack_inner(k_ref, w_ref, side_ref)
    first, last = edge_flags()
    mean, rate = moments(parts_ref, 16 * 4 * W)
    mean, gain, shift = mean[:1], rate[:1] * gain_ref[...], shift_ref[...]
    mean, gain, shift = (tile_lanes(v, 4) for v in (mean, gain, shift))
    keep_up = jnp.where(first, 0.0, 1.0)
    keep_down = jnp.where(last, 0.0, 1.0)
    for i in range(18):
        v = active(h_ref[i], mean, gain, shift)
        if i < 1:
            v = v * keep_up
        elif i >= 17:
            v = v * keep_down
        an[i] = v.astype(BF16)
    count = 4
    for f in range(0, 16, count):
        rows = [an[f + ky : f + ky + count].reshape(count * W, 512) for ky in range(3)]
        main = mm(jnp.concatenate(rows, axis=1), w_ref[...])
        side = mm(jnp.concatenate([v[:, 0:256] for v in rows], axis=1), side_ref[...])
        raw = x_ref[1 + f // 2 : 1 + f // 2 + count // 2].reshape(count // 2 * W, 512)
        skips = [mm(raw[:, 0:256], p_ref[...]), mm(raw[:, 256:512], p_ref[...])]
        skips = [
            jnp.concatenate([s[i // 2 * W : (i // 2 + 1) * W] for i in range(count)], axis=0) for s in skips
        ]
        cols = [main[:, o * 128 : (o + 1) * 128] + skips[o // 2] for o in range(4)]
        cols[0] = cols[0] + last_col(side[:, 0:128])
        cols[3] = cols[3] + next_col(side[:, 128:256])
        for i in range(count):
            for o in range(4):
                tmp[i, pl.ds(o, W, stride=4), :] = cols[o][i * W : (i + 1) * W]
            out_ref[:, f + i] = tmp[i].reshape(COLS, 32, 128).astype(BF16)


def swap(parts):
    return lax.all_to_all(parts, "rows", 0, 0, tiled=True)


def shape(*dims, dtype=BF16):
    return jax.ShapeDtypeStruct(dims, dtype)


def line(v):
    return v.reshape(1, -1)


def body(
    coarse,
    broad_entry_scale,
    broad_entry_bias,
    broad_entry_kernel,
    broad_inner_scale,
    broad_inner_bias,
    broad_inner_kernel,
    broad_skip_projection,
    detail_entry_scale,
    detail_entry_bias,
    detail_entry_kernel,
    detail_inner_scale,
    detail_inner_bias,
    detail_inner_kernel,
    detail_skip_projection,
):
    x = coarse.reshape(4, W, 512)
    stat = lambda c: shape(ROWS, 1, 2 * c, dtype=F32)
    parts, head, tail = call(
        coarse_stats_kernel, (stat(512), shape(2, W, 512), shape(2, W, 512)), name="coarse_stats"
    )(x)
    parts = swap(parts)
    up = lax.ppermute(tail, "rows", [(i, i + 1) for i in range(ROWS - 1)])
    down = lax.ppermute(head, "rows", [(i + 1, i) for i in range(ROWS - 1)])
    wide_h, parts = call(
        broad_entry_kernel_body,
        (shape(12, W, 512), stat(256)),
        [pltpu.VMEM((8, W, 512), BF16), pltpu.VMEM((2, 1024, 1024), BF16)],
        name="broad_entry",
        flops=1 << 32,
    )(x, up, down, parts, line(broad_entry_scale), line(broad_entry_bias), broad_entry_kernel)
    parts = swap(parts)
    wide_out, parts = call(
        broad_inner_kernel_body,
        (shape(10, W, 512), stat(256)),
        [pltpu.VMEM((12, W, 512), BF16)],
        name="broad_inner",
        flops=1 << 32,
    )(
        wide_h,
        x,
        up,
        down,
        parts,
        line(broad_inner_scale),
        line(broad_inner_bias),
        broad_inner_kernel.reshape(9 * 256, 256),
        broad_skip_projection,
    )
    parts = swap(parts)
    fine_h, parts = call(
        detail_entry_kernel_body,
        (shape(18, W, 512), stat(128)),
        [pltpu.VMEM((10, W, 512), BF16)] + [pltpu.VMEM((2, 2, 256, 256), BF16)] * 2,
        name="detail_entry",
        flops=1 << 32,
    )(wide_out, parts, line(detail_entry_scale), line(detail_entry_bias), detail_entry_kernel)
    parts = swap(parts)
    decoded = call(
        detail_inner_kernel_body,
        shape(COLS, 16, 32, 128),
        [
            pltpu.VMEM((18, W, 512), BF16),
            pltpu.VMEM((4, 4 * W, 128), F32),
            pltpu.VMEM((1536, 512), BF16),
            pltpu.VMEM((768, 256), BF16),
        ],
        name="detail_inner",
        flops=1 << 32,
    )(
        fine_h,
        wide_out,
        parts,
        line(detail_inner_scale),
        line(detail_inner_bias),
        detail_inner_kernel,
        detail_skip_projection,
    )
    return lax.all_to_all(decoded, "cols", 0, 0, tiled=True)


def solution(mesh):
    return jax.shard_map(
        body,
        mesh=mesh,
        in_specs=(P("cols", "rows", None, None),) + (P(),) * 14,
        out_specs=P(None, "rows", "cols", None),
        check_vma=False,
    )
```

```python
import functools

import jax
import jax.numpy as jnp
from jax import lax
from jax.experimental import pallas as pl
from jax.experimental.pallas import tpu as pltpu
from jax.sharding import PartitionSpec as P

GROUPS = 32
EPSILON = 1e-06
F32 = jnp.float32
BF16 = jnp.bfloat16
ROWS = 8
COLS = 16
W = 128
VMEM_LIMIT = 24 * 1024 * 1024


VMEM = pl.BlockSpec(memory_space=pltpu.VMEM)
HBM = pl.BlockSpec(memory_space=pltpu.HBM)


def call(kernel, out_shape, scratch=(), flops=0, name=None, specs=None):
    return pl.pallas_call(
        kernel,
        out_shape=out_shape,
        **({} if specs is None else {"in_specs": specs}),
        scratch_shapes=list(scratch),
        name=name,
        cost_estimate=pl.CostEstimate(flops=flops, bytes_accessed=0, transcendentals=0),
        compiler_params=pltpu.CompilerParams(vmem_limit_bytes=VMEM_LIMIT),
    )


def group_sum(v, size):
    count = v.shape[-1]
    lane = lax.broadcasted_iota(jnp.int32, v.shape, 1)
    step = 1
    while step < size:
        before = pltpu.roll(v, step, 1)
        after = pltpu.roll(v, count - step, 1)
        v = v + jnp.where((lane & step) != 0, before, after)
        step *= 2
    return v


def moments(parts, held):
    both = jnp.concatenate([parts[d] for d in range(ROWS)], axis=0)
    chans = both.shape[1] // 2
    size = chans // GROUPS
    sums, squares = both[:, :chans], both[:, chans:]
    entries = float(ROWS * held * size)
    total = jnp.broadcast_to(jnp.sum(sums, axis=0, keepdims=True), sums.shape)
    mean = group_sum(total, size) / entries
    off = sums / float(held) - mean
    spread = jnp.sum(squares + float(held) * off * off, axis=0, keepdims=True)
    spread = group_sum(jnp.broadcast_to(spread, sums.shape), size) / entries
    return mean, lax.rsqrt(spread + EPSILON)


def tile_lanes(v, times):
    return jnp.concatenate([v] * times, axis=1) if times > 1 else v


def active(value, mean, gain, shift):
    y = (value.astype(F32) - mean) * gain + shift
    half = 0.5 * y
    return half + half * jnp.tanh(half)


def block_moments(blocks):
    n = blocks[0].shape[0]
    sums, squares = [], []
    for block in blocks:
        s = jnp.sum(block, axis=0, keepdims=True)
        d = block - s / float(n)
        sums.append(s)
        squares.append(jnp.sum(d * d, axis=0, keepdims=True))
    return merge_moments(sums, squares, n)


def merge_moments(sums, squares, n):
    total = functools.reduce(jnp.add, sums)
    mean = total / float(n * len(sums))
    out = functools.reduce(jnp.add, squares)
    for s in sums:
        off = s / float(n) - mean
        out = out + float(n) * off * off
    return jnp.concatenate([total, out], axis=1)


def publish(ref, vector):
    for d in range(ROWS):
        ref[d] = vector


def next_col(v):
    col = lax.broadcasted_iota(jnp.int32, v.shape, 0) % W
    return jnp.where(col == W - 1, 0.0, pltpu.roll(v, v.shape[0] - 1, 0))


def last_col(v):
    col = lax.broadcasted_iota(jnp.int32, v.shape, 0) % W
    return jnp.where(col == 0, 0.0, pltpu.roll(v, 1, 0))


def edge_flags():
    row = lax.axis_index("rows")
    return row == 0, row == ROWS - 1


def mm(a, b):
    return jnp.dot(a, b, preferred_element_type=F32)


def coarse_stats_kernel(x_ref, out_ref, head_ref, tail_ref):
    x = x_ref[...].astype(F32).reshape(4 * W, 512)
    head_ref[...] = x_ref[0:2]
    tail_ref[...] = x_ref[2:4]
    publish(out_ref, block_moments([x]))


def pack_broad(k_ref, out_ref):
    rows = (((0,), (1, 2)), ((0, 1), (2,)))
    step = 128
    for a in range(2):
        for t in range(2):
            for c in range(0, 512, step):
                col = [
                    functools.reduce(
                        jnp.add, [k_ref[ky, kx, c : c + step, :].astype(F32) for ky in rows[a][t]]
                    )
                    for kx in range(3)
                ]
                for n, v in enumerate((col[0], col[1] + col[2], col[0] + col[1], col[2])):
                    out_ref[a, t * 512 + c : t * 512 + c + step, n * 256 : (n + 1) * 256] = v.astype(BF16)


def pack_detail(k_ref, x_ref, z_ref):
    rows = (((0,), (1, 2)), ((0, 1), (2,)))
    for a in range(2):
        for t in range(2):
            col = [
                functools.reduce(jnp.add, [k_ref[ky, kx].astype(F32) for ky in rows[a][t]])
                for kx in range(3)
            ]
            x_ref[a, t] = jnp.concatenate([col[0] + col[1], col[0]], axis=1).astype(BF16)
            z_ref[a, t] = jnp.concatenate([col[2], col[1] + col[2]], axis=1).astype(BF16)


def pack_inner(k_ref, main_ref, side_ref):
    zero = jnp.zeros((128, 128), BF16)
    for ky in range(3):
        k = [k_ref[ky, kx] for kx in range(3)]
        table = (
            (zero, zero, k[2], k[1]),
            (k[1], k[0], zero, zero),
            (k[2], k[1], k[0], zero),
            (zero, k[2], k[1], k[0]),
        )
        for i, line in enumerate(table):
            for o, v in enumerate(line):
                main_ref[ky * 512 + i * 128 : ky * 512 + (i + 1) * 128, o * 128 : (o + 1) * 128] = v
        base = ky * 256
        side_ref[base : base + 128, 0:128] = k[0]
        side_ref[base : base + 128, 128:256] = zero
        side_ref[base + 128 : base + 256, 0:128] = zero
        side_ref[base + 128 : base + 256, 128:256] = k[2]


def prepare_kernel_body(
    parts_ref, gain_hbm, shift_hbm, k_hbm, parts_out, gain_ref, shift_ref, w_ref, k_ref, sems
):
    pairs = ((gain_hbm, gain_ref), (shift_hbm, shift_ref)) + tuple((k_hbm.at[i], k_ref.at[i]) for i in range(3))
    copies = [pltpu.make_async_copy(src, dst, sems.at[i]) for i, (src, dst) in enumerate(pairs)]
    for copy in copies:
        copy.start()
    for d in range(ROWS):
        parts_out[d] = parts_ref[d]
    for copy in copies:
        copy.wait()
    pack_broad(k_ref, w_ref)


def broad_entry_kernel_body(
    x_ref, up_ref, down_ref, parts_ref, gain_ref, shift_ref, w_ref, out_ref, stat_ref, an
):
    first, last = edge_flags()
    mean, rate = moments(parts_ref, 4 * W)
    mean, gain, shift = mean[:1], rate[:1] * gain_ref[...], shift_ref[...]
    keep_up = jnp.where(first, 0.0, 1.0)
    keep_down = jnp.where(last, 0.0, 1.0)
    for h in range(2):
        an[h] = (active(up_ref[h], mean, gain, shift) * keep_up).astype(BF16)
        an[6 + h] = (active(down_ref[h], mean, gain, shift) * keep_down).astype(BF16)
    for h in range(4):
        an[2 + h] = active(x_ref[h], mean, gain, shift).astype(BF16)
    blocks = []
    for a in range(2):
        near = an[a : a + 6].reshape(6 * W, 512)
        far = an[a + 1 : a + 7].reshape(6 * W, 512)
        both = jnp.concatenate([near, far], axis=1)
        for b in range(2):
            z = [mm(both, w_ref[a, :, n * 256 : (n + 1) * 256]) for n in (2 * b, 2 * b + 1)]
            v = last_col(z[0]) + z[1] if b == 0 else z[0] + next_col(z[1])
            v = v.astype(BF16)
            for h in range(6):
                out_ref[2 * h + a, :, b * 256 : (b + 1) * 256] = v[h * W : (h + 1) * W]
            blocks.append(v[W : 5 * W].astype(F32))
    publish(stat_ref, block_moments(blocks))


def broad_inner_kernel_body(
    h_ref, x_ref, up_ref, down_ref, parts_ref, gain_ref, shift_ref, w_ref, p_ref, out_ref, stat_ref, an
):
    first, last = edge_flags()
    mean, rate = moments(parts_ref, 8 * 2 * W)
    mean, gain, shift = mean[:1], rate[:1] * gain_ref[...], shift_ref[...]
    mean, gain, shift = (tile_lanes(v, 2) for v in (mean, gain, shift))
    keep_up = jnp.where(first, 0.0, 1.0)
    keep_down = jnp.where(last, 0.0, 1.0)
    for i in range(12):
        v = active(h_ref[i], mean, gain, shift)
        if i < 2:
            v = v * keep_up
        elif i >= 10:
            v = v * keep_down
        an[i] = v.astype(BF16)
    skip_in = jnp.concatenate([up_ref[1]] + [x_ref[h] for h in range(4)] + [down_ref[0]], axis=0)
    skip = mm(skip_in, p_ref[...])
    w = w_ref
    even_w = jnp.concatenate([w[ky * 768 + 256 : ky * 768 + 768] for ky in range(3)], axis=0)
    odd_w = jnp.concatenate([w[ky * 768 : ky * 768 + 512] for ky in range(3)], axis=0)
    even_side = jnp.concatenate([w[ky * 768 : ky * 768 + 256] for ky in range(3)], axis=0)
    odd_side = jnp.concatenate([w[ky * 768 + 512 : ky * 768 + 768] for ky in range(3)], axis=0)
    evens, odds = [], []
    count = 5
    for j in range(0, 10, count):
        main = jnp.concatenate([an[j + ky : j + ky + count].reshape(count * W, 512) for ky in range(3)], axis=1)
        even_in = jnp.concatenate(
            [an[j + ky : j + ky + count, :, 0:256].reshape(count * W, 256) for ky in range(3)], axis=1
        )
        odd_in = jnp.concatenate(
            [an[j + ky : j + ky + count, :, 256:512].reshape(count * W, 256) for ky in range(3)], axis=1
        )
        extra = jnp.concatenate([skip[(i + 1) // 2 * W : ((i + 1) // 2 + 1) * W] for i in range(j, j + count)], axis=0)
        even = (mm(main, even_w) + last_col(mm(odd_in, even_side)) + extra).astype(BF16)
        odd = (mm(main, odd_w) + next_col(mm(even_in, odd_side)) + extra).astype(BF16)
        for i in range(count):
            out_ref[j + i, :, 0:256] = even[i * W : (i + 1) * W]
            out_ref[j + i, :, 256:512] = odd[i * W : (i + 1) * W]
        lo, hi = (W, count * W) if j == 0 else (0, (count - 1) * W)
        evens.append(even[lo:hi].astype(F32))
        odds.append(odd[lo:hi].astype(F32))
    publish(stat_ref, block_moments(evens + odds))


def detail_entry_kernel_body(x_ref, parts_ref, gain_ref, shift_ref, k_ref, out_ref, stat_ref, an, wx_ref, wz_ref):
    pack_detail(k_ref, wx_ref, wz_ref)
    first, last = edge_flags()
    mean, rate = moments(parts_ref, 8 * 2 * W)
    mean, gain, shift = mean[:1], rate[:1] * gain_ref[...], shift_ref[...]
    mean, gain, shift = (tile_lanes(v, 2) for v in (mean, gain, shift))
    keep_up = jnp.where(first, 0.0, 1.0)
    keep_down = jnp.where(last, 0.0, 1.0)
    for i in range(10):
        v = active(x_ref[i], mean, gain, shift)
        if i < 1:
            v = v * keep_up
        elif i >= 9:
            v = v * keep_down
        an[i] = v.astype(BF16)
    blocks = []
    for a in range(2):
        lhs = [an[t : t + 9].reshape(9 * W, 512) for t in range(2)]
        main = jnp.concatenate(lhs, axis=1)
        odd = jnp.concatenate([v[:, 256:512] for v in lhs], axis=1)
        even = jnp.concatenate([v[:, 0:256] for v in lhs], axis=1)
        wx = [wx_ref[a, t] for t in range(2)]
        wz = [wz_ref[a, t] for t in range(2)]
        middle = mm(main, jnp.concatenate([wx[0], wz[0], wx[1], wz[1]], axis=0))
        right = mm(odd, jnp.concatenate(wx, axis=0))
        left = mm(even, jnp.concatenate(wz, axis=0))
        q3 = (right[:, 0:128] + next_col(left[:, 0:128])).astype(BF16)
        q0 = (last_col(right[:, 128:256]) + left[:, 128:256]).astype(BF16)
        middle = middle.astype(BF16)
        for i in range(9):
            f = 2 * i + 1 - a
            out_ref[f, :, 0:128] = q3[i * W : (i + 1) * W]
            out_ref[f, :, 128:256] = q0[i * W : (i + 1) * W]
            out_ref[f, :, 256:512] = middle[i * W : (i + 1) * W]
        lo, hi = (W, 9 * W) if a == 1 else (0, 8 * W)
        for v in (q3, q0, middle[:, 0:128], middle[:, 128:256]):
            blocks.append(v[lo:hi].astype(F32))
    publish(stat_ref, block_moments(blocks))


def detail_inner_kernel_body(
    h_ref, x_ref, parts_ref, gain_ref, shift_ref, k_ref, p_ref, out_ref, an, tmp, w_ref, side_ref
):
    pack_inner(k_ref, w_ref, side_ref)
    first, last = edge_flags()
    mean, rate = moments(parts_ref, 16 * 4 * W)
    mean, gain, shift = mean[:1], rate[:1] * gain_ref[...], shift_ref[...]
    mean, gain, shift = (tile_lanes(v, 4) for v in (mean, gain, shift))
    keep_up = jnp.where(first, 0.0, 1.0)
    keep_down = jnp.where(last, 0.0, 1.0)
    for i in range(18):
        v = active(h_ref[i], mean, gain, shift)
        if i < 1:
            v = v * keep_up
        elif i >= 17:
            v = v * keep_down
        an[i] = v.astype(BF16)
    count = 4
    for f in range(0, 16, count):
        rows = [an[f + ky : f + ky + count].reshape(count * W, 512) for ky in range(3)]
        main = mm(jnp.concatenate(rows, axis=1), w_ref[...])
        side = mm(jnp.concatenate([v[:, 0:256] for v in rows], axis=1), side_ref[...])
        raw = x_ref[1 + f // 2 : 1 + f // 2 + count // 2].reshape(count // 2 * W, 512)
        skips = [mm(raw[:, 0:256], p_ref[...]), mm(raw[:, 256:512], p_ref[...])]
        skips = [
            jnp.concatenate([s[i // 2 * W : (i // 2 + 1) * W] for i in range(count)], axis=0) for s in skips
        ]
        cols = [main[:, o * 128 : (o + 1) * 128] + skips[o // 2] for o in range(4)]
        cols[0] = cols[0] + last_col(side[:, 0:128])
        cols[3] = cols[3] + next_col(side[:, 128:256])
        for i in range(count):
            for o in range(4):
                tmp[i, pl.ds(o, W, stride=4), :] = cols[o][i * W : (i + 1) * W]
            out_ref[:, f + i] = tmp[i].reshape(COLS, 32, 128).astype(BF16)


def swap(parts):
    return lax.all_to_all(parts, "rows", 0, 0, tiled=True)


def shape(*dims, dtype=BF16):
    return jax.ShapeDtypeStruct(dims, dtype)


def stay(v):
    return pltpu.with_memory_space_constraint(v, pltpu.HBM)


def line(v):
    return v.reshape(1, -1)


def body(
    coarse,
    broad_entry_scale,
    broad_entry_bias,
    broad_entry_kernel,
    broad_inner_scale,
    broad_inner_bias,
    broad_inner_kernel,
    broad_skip_projection,
    detail_entry_scale,
    detail_entry_bias,
    detail_entry_kernel,
    detail_inner_scale,
    detail_inner_bias,
    detail_inner_kernel,
    detail_skip_projection,
):
    x = coarse.reshape(4, W, 512)
    stat = lambda c: shape(ROWS, 1, 2 * c, dtype=F32)
    parts, head, tail = call(
        coarse_stats_kernel, (stat(512), shape(2, W, 512), shape(2, W, 512)), name="coarse_stats"
    )(x)
    up = lax.ppermute(tail, "rows", [(i, (i + 1) % ROWS) for i in range(ROWS)])
    down = lax.ppermute(head, "rows", [((i + 1) % ROWS, i) for i in range(ROWS)])
    parts, gain, shift, packed = call(
        prepare_kernel_body,
        (stat(512), shape(1, 512, dtype=F32), shape(1, 512, dtype=F32), shape(2, 1024, 1024)),
        [pltpu.VMEM((3, 3, 512, 256), BF16), pltpu.SemaphoreType.DMA((5,))],
        name="prepare",
        flops=1 << 30,
        specs=[VMEM] + [HBM] * 3,
    )(parts, *(stay(v) for v in (line(broad_entry_scale), line(broad_entry_bias), broad_entry_kernel)))
    parts = swap(parts)
    wide_h, parts = call(
        broad_entry_kernel_body,
        (shape(12, W, 512), stat(256)),
        [pltpu.VMEM((8, W, 512), BF16)],
        name="broad_entry",
        flops=1 << 32,
    )(x, up, down, parts, gain, shift, packed)
    parts = swap(parts)
    wide_out, parts = call(
        broad_inner_kernel_body,
        (shape(10, W, 512), stat(256)),
        [pltpu.VMEM((12, W, 512), BF16)],
        name="broad_inner",
        flops=1 << 32,
    )(
        wide_h,
        x,
        up,
        down,
        parts,
        line(broad_inner_scale),
        line(broad_inner_bias),
        broad_inner_kernel.reshape(9 * 256, 256),
        broad_skip_projection,
    )
    parts = swap(parts)
    fine_h, parts = call(
        detail_entry_kernel_body,
        (shape(18, W, 512), stat(128)),
        [pltpu.VMEM((10, W, 512), BF16)] + [pltpu.VMEM((2, 2, 256, 256), BF16)] * 2,
        name="detail_entry",
        flops=1 << 32,
    )(wide_out, parts, line(detail_entry_scale), line(detail_entry_bias), detail_entry_kernel)
    parts = swap(parts)
    decoded = call(
        detail_inner_kernel_body,
        shape(COLS, 16, 32, 128),
        [
            pltpu.VMEM((18, W, 512), BF16),
            pltpu.VMEM((4, 4 * W, 128), F32),
            pltpu.VMEM((1536, 512), BF16),
            pltpu.VMEM((768, 256), BF16),
        ],
        name="detail_inner",
        flops=1 << 32,
    )(
        fine_h,
        wide_out,
        parts,
        line(detail_inner_scale),
        line(detail_inner_bias),
        detail_inner_kernel,
        detail_skip_projection,
    )
    return lax.all_to_all(decoded, "cols", 0, 0, tiled=True)


def solution(mesh):
    return jax.shard_map(
        body,
        mesh=mesh,
        in_specs=(P("cols", "rows", None, None),) + (P(),) * 14,
        out_specs=P(None, "rows", "cols", None),
        check_vma=False,
    )
```

```python
import functools

import jax
import jax.numpy as jnp
from jax import lax
from jax.experimental import pallas as pl
from jax.experimental.pallas import tpu as pltpu
from jax.sharding import PartitionSpec as P

GROUPS = 32
EPSILON = 1e-06
F32 = jnp.float32
BF16 = jnp.bfloat16
ROWS = 8
COLS = 16
W = 128
VMEM_LIMIT = 24 * 1024 * 1024


VMEM = pl.BlockSpec(memory_space=pltpu.VMEM)
HBM = pl.BlockSpec(memory_space=pltpu.HBM)


def call(kernel, out_shape, scratch=(), flops=0, name=None, specs=None):
    return pl.pallas_call(
        kernel,
        out_shape=out_shape,
        **({} if specs is None else {"in_specs": specs}),
        scratch_shapes=list(scratch),
        name=name,
        cost_estimate=pl.CostEstimate(flops=flops, bytes_accessed=0, transcendentals=0),
        compiler_params=pltpu.CompilerParams(vmem_limit_bytes=VMEM_LIMIT),
    )


def group_sum(v, size):
    count = v.shape[-1]
    lane = lax.broadcasted_iota(jnp.int32, v.shape, 1)
    step = 1
    while step < size:
        before = pltpu.roll(v, step, 1)
        after = pltpu.roll(v, count - step, 1)
        v = v + jnp.where((lane & step) != 0, before, after)
        step *= 2
    return v


def moments(parts, held):
    lines = []
    for ref in parts:
        lines += [ref[d] for d in range(ref.shape[0])] if len(ref.shape) == 3 else [ref[...]]
    both = jnp.concatenate(lines, axis=0)
    chans = both.shape[1] // 2
    size = chans // GROUPS
    sums, squares = both[:, :chans], both[:, chans:]
    entries = float(ROWS * held * size)
    total = jnp.broadcast_to(jnp.sum(sums, axis=0, keepdims=True), sums.shape)
    mean = group_sum(total, size) / entries
    off = sums / float(held) - mean
    spread = jnp.sum(squares + float(held) * off * off, axis=0, keepdims=True)
    spread = group_sum(jnp.broadcast_to(spread, sums.shape), size) / entries
    return mean, lax.rsqrt(spread + EPSILON)


def tile_lanes(v, times):
    return jnp.concatenate([v] * times, axis=1) if times > 1 else v


def active(value, mean, gain, shift):
    half = (value.astype(F32) - mean) * gain + shift
    return half + half * jnp.tanh(half)


def block_moments(blocks):
    sums, squares, sizes = [], [], []
    for block in blocks:
        n = block.shape[0]
        if n == 0:
            continue
        origin = jnp.mean(block[0:16], axis=0, keepdims=True)
        d = block - origin
        s = jnp.sum(d, axis=0, keepdims=True)
        q = jnp.sum(d * d, axis=0, keepdims=True)
        sums.append(s + float(n) * origin)
        squares.append(jnp.maximum(q - s * s / float(n), 0.0))
        sizes.append(n)
    total = functools.reduce(jnp.add, sums)
    mean = total / float(sum(sizes))
    out = functools.reduce(jnp.add, squares)
    for s, n in zip(sums, sizes):
        off = s / float(n) - mean
        out = out + float(n) * off * off
    return jnp.concatenate([total, out], axis=1)


def publish(ref, vector):
    for d in range(ROWS):
        ref[d] = vector


def next_col(v):
    col = lax.broadcasted_iota(jnp.int32, v.shape, 0) % W
    return jnp.where(col == W - 1, 0.0, pltpu.roll(v, v.shape[0] - 1, 0))


def last_col(v):
    col = lax.broadcasted_iota(jnp.int32, v.shape, 0) % W
    return jnp.where(col == 0, 0.0, pltpu.roll(v, 1, 0))


def edge_flags():
    row = lax.axis_index("rows")
    return row == 0, row == ROWS - 1


def mm(a, b):
    return jnp.dot(a, b, preferred_element_type=F32)


def coarse_stats_kernel(x_ref, out_ref, head_ref, tail_ref):
    x = x_ref[...].astype(F32).reshape(4 * W, 512)
    head_ref[...] = x_ref[0:2]
    tail_ref[...] = x_ref[2:4]
    publish(out_ref, block_moments([x]))


def pack_broad(k_ref, out_ref):
    rows = (((0,), (1, 2)), ((0, 1), (2,)))
    step = 128
    for a in range(2):
        for t in range(2):
            for c in range(0, 512, step):
                col = [
                    functools.reduce(
                        jnp.add, [k_ref[ky, kx, c : c + step, :].astype(F32) for ky in rows[a][t]]
                    )
                    for kx in range(3)
                ]
                for n, v in enumerate((col[0], col[1] + col[2], col[0] + col[1], col[2])):
                    out_ref[a, t * 512 + c : t * 512 + c + step, n * 256 : (n + 1) * 256] = v.astype(BF16)


def pack_detail(k_ref, x_ref, z_ref):
    rows = (((0,), (1, 2)), ((0, 1), (2,)))
    for a in range(2):
        for t in range(2):
            col = [
                functools.reduce(jnp.add, [k_ref[ky, kx].astype(F32) for ky in rows[a][t]])
                for kx in range(3)
            ]
            x_ref[a, t] = jnp.concatenate([col[0] + col[1], col[0]], axis=1).astype(BF16)
            z_ref[a, t] = jnp.concatenate([col[2], col[1] + col[2]], axis=1).astype(BF16)


def prepare_kernel_body(
    parts_ref, gain_hbm, shift_hbm, k_hbm, parts_out, gain_ref, shift_ref, w_ref, k_ref, sems
):
    pairs = ((gain_hbm, gain_ref), (shift_hbm, shift_ref)) + tuple((k_hbm.at[i], k_ref.at[i]) for i in range(3))
    copies = [pltpu.make_async_copy(src, dst, sems.at[i]) for i, (src, dst) in enumerate(pairs)]
    for copy in copies:
        copy.start()
    for d in range(ROWS):
        parts_out[d] = parts_ref[d]
    for copy in copies:
        copy.wait()
    pack_broad(k_ref, w_ref)


def broad_entry_kernel_body(
    x_ref, up_ref, down_ref, parts_ref, gain_ref, shift_ref, w_ref, out_ref, stat_ref, an
):
    first, last = edge_flags()
    mean, rate = moments([parts_ref], 4 * W)
    mean, gain, shift = mean[:1], 0.5 * rate[:1] * gain_ref[...], 0.5 * shift_ref[...]
    keep_up = jnp.where(first, 0.0, 1.0)
    keep_down = jnp.where(last, 0.0, 1.0)
    def norm(h):
        if h < 2:
            v = active(up_ref[h], mean, gain, shift) * keep_up
        elif h < 6:
            v = active(x_ref[h - 2], mean, gain, shift)
        else:
            v = active(down_ref[h - 6], mean, gain, shift) * keep_down
        an[h] = v.astype(BF16)

    ready, blocks, count = 0, [], 1
    for start in range(0, 6, count):
        while ready < start + count + 2:
            norm(ready)
            ready += 1
        lo, hi = max(start, 1) - start, min(start + count, 5) - start
        for a in range(2):
            near = an[start + a : start + a + count].reshape(count * W, 512)
            far = an[start + a + 1 : start + a + 1 + count].reshape(count * W, 512)
            both = jnp.concatenate([near, far], axis=1)
            for b in range(2):
                z = [mm(both, w_ref[a, :, n * 256 : (n + 1) * 256]) for n in (2 * b, 2 * b + 1)]
                v = last_col(z[0]) + z[1] if b == 0 else z[0] + next_col(z[1])
                for h in range(count):
                    out_ref[2 * (start + h) + a, :, b * 256 : (b + 1) * 256] = v[h * W : (h + 1) * W].astype(BF16)
                blocks.append(v[lo * W : hi * W])
    publish(stat_ref, block_moments(blocks))


def broad_inner_kernel_body(
    h_ref, x_ref, up_ref, down_ref, parts_ref, gain_ref, shift_ref, w_ref, p_ref,
    out_ref, send_ref, stat_ref, an, odd_line, even_line, rim,
):
    first, last = edge_flags()
    mean, rate = moments([parts_ref], 8 * 2 * W)
    mean, gain, shift = mean[:1], 0.5 * rate[:1] * gain_ref[...], 0.5 * shift_ref[...]
    mean, gain, shift = (tile_lanes(v, 2) for v in (mean, gain, shift))
    keep_up = jnp.where(first, 0.0, 1.0)
    keep_down = jnp.where(last, 0.0, 1.0)
    for i in range(12):
        v = active(h_ref[i], mean, gain, shift)
        if i < 2:
            v = v * keep_up
        elif i >= 10:
            v = v * keep_down
        an[i] = v.astype(BF16)
    skip_in = jnp.concatenate([up_ref[1]] + [x_ref[h] for h in range(4)] + [down_ref[0]], axis=0)
    skip = mm(skip_in, p_ref[...])
    w = w_ref
    even_w = jnp.concatenate([w[ky * 768 + 256 : ky * 768 + 768] for ky in range(3)], axis=0)
    odd_w = jnp.concatenate([w[ky * 768 : ky * 768 + 512] for ky in range(3)], axis=0)
    even_side = jnp.concatenate([w[ky * 768 : ky * 768 + 256] for ky in range(3)], axis=0)
    odd_side = jnp.concatenate([w[ky * 768 + 512 : ky * 768 + 768] for ky in range(3)], axis=0)
    evens, odds = [], []
    even_line[...] = jnp.zeros(even_line.shape, F32)
    rim[...] = jnp.zeros(rim.shape, F32)
    count = 5
    for j in range(0, 10, count):
        main = jnp.concatenate([an[j + ky : j + ky + count].reshape(count * W, 512) for ky in range(3)], axis=1)
        even_in = jnp.concatenate(
            [an[j + ky : j + ky + count, :, 0:256].reshape(count * W, 256) for ky in range(3)], axis=1
        )
        odd_in = jnp.concatenate(
            [an[j + ky : j + ky + count, :, 256:512].reshape(count * W, 256) for ky in range(3)], axis=1
        )
        extra = jnp.concatenate([skip[(i + 1) // 2 * W : ((i + 1) // 2 + 1) * W] for i in range(j, j + count)], axis=0)
        even = mm(main, even_w) + last_col(mm(odd_in, even_side)) + extra
        odd = mm(main, odd_w) + next_col(mm(even_in, odd_side)) + extra
        before = last_col(odd)
        for i in range(count):
            e, o, p = (v[i * W : (i + 1) * W] for v in (even, odd, before))
            out_ref[j + i, :, 0:256] = e.astype(BF16)
            out_ref[j + i, :, 256:512] = o.astype(BF16)
            block = jnp.concatenate([p.reshape(COLS, 8, 256), e.reshape(COLS, 8, 256)], axis=1)
            send_ref[:, (j + i) * 16 : (j + i + 1) * 16, :] = block.astype(BF16)
            for n in range(2):
                odd_line[i, n] = o[:, n * 128 : (n + 1) * 128]
                even_line[i, n, 0:W] = e[:, n * 128 : (n + 1) * 128]
                rim[n, pl.ds(j + i, COLS, stride=24), :] = odd_line[i, n, pl.ds(7, COLS, stride=8), :]
                rim[n, pl.ds(10 + j + i, COLS, stride=24), :] = even_line[i, n, pl.ds(8, COLS, stride=8), :]
        lo, hi = (W, count * W) if j == 0 else (0, (count - 1) * W)
        evens.append(even[lo:hi])
        odds.append(odd[lo:hi])
    for n in range(2):
        send_ref[:, 160:184, n * 128 : (n + 1) * 128] = rim[n].reshape(COLS, 24, 128).astype(BF16)
    stat_ref[...] = block_moments(evens + odds)


def detail_stats_kernel_body(
    x_ref, a_ref, b_ref, c_ref, d_ref, gain_ref, shift_ref, k_ref, stat_ref, norm_ref, an, wx_ref, wz_ref
):
    pack_detail(k_ref, wx_ref, wz_ref)
    first, last = edge_flags()
    mean, rate = moments([a_ref, b_ref, c_ref, d_ref], 8 * 2 * W)
    norm_ref[...] = jnp.concatenate([mean[:1], rate[:1]], axis=1)
    mean, gain, shift = mean[:1], 0.5 * rate[:1] * gain_ref[...], 0.5 * shift_ref[...]
    mean, gain, shift = (tile_lanes(v, 2) for v in (mean, gain, shift))
    keep_up = jnp.where(first, 0.0, 1.0)
    keep_down = jnp.where(last, 0.0, 1.0)
    for i in range(10):
        v = active(x_ref[i], mean, gain, shift)
        if i < 1:
            v = v * keep_up
        elif i >= 9:
            v = v * keep_down
        an[i] = v.astype(BF16)
    blocks = []
    for a in range(2):
        lhs = [an[a + t : a + t + 8].reshape(8 * W, 512) for t in range(2)]
        main = jnp.concatenate(lhs, axis=1)
        odd = jnp.concatenate([v[:, 256:512] for v in lhs], axis=1)
        even = jnp.concatenate([v[:, 0:256] for v in lhs], axis=1)
        wx = [wx_ref[a, t] for t in range(2)]
        wz = [wz_ref[a, t] for t in range(2)]
        middle = mm(main, jnp.concatenate([wx[0], wz[0], wx[1], wz[1]], axis=0))
        right = mm(odd, jnp.concatenate(wx, axis=0))
        left = mm(even, jnp.concatenate(wz, axis=0))
        q3 = right[:, 0:128] + next_col(left[:, 0:128])
        q0 = last_col(right[:, 128:256]) + left[:, 128:256]
        for v in (q3, q0, middle[:, 0:128], middle[:, 128:256]):
            blocks.append(v)
    stat_ref[...] = block_moments(blocks)


def summary_kernel_body(here_ref, there_ref, norm_ref, out_ref):
    mean, rate = moments([here_ref, there_ref], 16 * 4 * W)
    both = jnp.concatenate([mean[:1], rate[:1], norm_ref[...]], axis=1)
    for c in range(COLS):
        out_ref[c] = both


def pixel(j, u):
    if u == 15:
        return 160 + j
    if u == 16:
        return 170 + j
    return j * 16 + (8 + u // 2 if u % 2 == 0 else (u + 1) // 2)


def detail_kernel_body(
    x_ref, norm_ref, gain3_ref, shift3_ref, gain4_ref, shift4_ref, k3_ref, k4_ref, p_ref,
    out_ref, an3, an4, wx_ref, wz_ref, w_ref, tmp,
):
    step = pl.program_id(0)

    @pl.when(step == 0)
    def _():
        pack_detail(k3_ref, wx_ref, wz_ref)
        zero = jnp.zeros((128, 128), BF16)
        for ky in range(3):
            k = [k4_ref[ky, kx] for kx in range(3)]
            table = ((k[0], zero), (k[1], k[0]), (k[2], k[1]), (zero, k[2]))
            for i, pair in enumerate(table):
                at = ky * 512 + i * 128
                w_ref[at : at + 128, 0:128] = pair[0]
                w_ref[at : at + 128, 128:256] = pair[1]
        first, last = edge_flags()
        keep_up = jnp.where(first, 0.0, 1.0)
        keep_down = jnp.where(last, 0.0, 1.0)
        col = lax.axis_index("cols")
        keep_left = jnp.where(col == 0, 0.0, 1.0)
        keep_right = jnp.where(col == COLS - 1, 0.0, 1.0)
        norm = jnp.concatenate([norm_ref[i] for i in range(COLS)], axis=0)
        mean4, rate4 = (tile_lanes(norm[:, n * 128 : (n + 1) * 128], 2) for n in range(2))
        mean3, rate3 = norm[:, 256:512], norm[:, 512:768]
        gain3, shift3 = 0.5 * rate3 * gain3_ref[...], 0.5 * shift3_ref[...]
        gain4, shift4 = 0.5 * rate4 * tile_lanes(gain4_ref[...], 2), 0.5 * tile_lanes(shift4_ref[...], 2)
        for j in range(10):
            for u in range(-1, 17):
                v = active(x_ref[pixel(j, u)], mean3, gain3, shift3)
                if j == 0:
                    v = v * keep_up
                elif j == 9:
                    v = v * keep_down
                if u == -1:
                    v = v * keep_left
                elif u == 16:
                    v = v * keep_right
                an3[j, (u + 1) * 16 : (u + 2) * 16] = v.astype(BF16)
        size = 17 * 16
        count = 3
        lane = lax.broadcasted_iota(jnp.int32, (16, 256), 1)
        left_mask = jnp.where(lane < 128, keep_left, 1.0)
        right_mask = jnp.where(lane >= 128, keep_right, 1.0)
        for a in range(2):
            w = jnp.concatenate([wx_ref[a, 0], wz_ref[a, 0], wx_ref[a, 1], wz_ref[a, 1]], axis=0)
            for i in range(0, 9, count):
                lhs = jnp.concatenate(
                    [
                        an3[i + t : i + t + count, s : s + size].reshape(count * size, 256)
                        for t in range(2)
                        for s in (0, 16)
                    ],
                    axis=1,
                )
                v = mm(lhs, w).astype(BF16).reshape(count * 17, 16, 256)
                v = active(v, mean4, gain4, shift4)
                for n in range(count):
                    f = 2 * (i + n) + 1 - a
                    line = v[n * 17 : (n + 1) * 17]
                    if f == 0:
                        line = line * keep_up
                    elif f == 17:
                        line = line * keep_down
                    an4[f, 16 : size - 16] = line[1:16].reshape(15 * 16, 256).astype(BF16)
                    an4[f, 0:16] = (line[0] * left_mask).astype(BF16)
                    an4[f, size - 16 : size] = (line[16] * right_mask).astype(BF16)

    count = 4
    base = step * count
    lhs = jnp.concatenate(
        [an4[pl.ds(base + ky, count), s : s + 256].reshape(count * 256, 256) for ky in range(3) for s in (0, 16)],
        axis=1,
    )
    v = mm(lhs, w_ref[...])
    raw = []
    for n in range(count // 2):
        j = step * (count // 2) + n + 1
        raw += [x_ref[160 + j if u == 15 else j * 16 + (8 + u // 2 if u % 2 == 0 else (u + 1) // 2)] for u in range(16)]
    skip = mm(jnp.concatenate(raw, axis=0), p_ref[...])
    for n in range(count):
        for b in range(2):
            part = v[n * 256 : (n + 1) * 256, b * 128 : (b + 1) * 128] + skip[n // 2 * 256 : (n // 2 + 1) * 256]
            for u in range(16):
                at = (2 * u + b) * 16
                tmp[n, at : at + 16] = part[u * 16 : (u + 1) * 16]
        for image in range(16):
            out_ref[image, n] = tmp[n, pl.ds(image, 32, stride=16), :].astype(BF16)


def swap(parts):
    return lax.all_to_all(parts, "rows", 0, 0, tiled=True)


def across_z(v):
    return lax.ppermute(v, "rows", [(i, i ^ 1) for i in range(ROWS)])


def along_y(v):
    return [lax.ppermute(v, "rows", [(i, (i + 2 * k) % ROWS) for i in range(ROWS)]) for k in range(1, 4)]


def shape(*dims, dtype=BF16):
    return jax.ShapeDtypeStruct(dims, dtype)


def stay(v):
    return pltpu.with_memory_space_constraint(v, pltpu.HBM)


def line(v):
    return v.reshape(1, -1)


def body(
    coarse,
    broad_entry_scale,
    broad_entry_bias,
    broad_entry_kernel,
    broad_inner_scale,
    broad_inner_bias,
    broad_inner_kernel,
    broad_skip_projection,
    detail_entry_scale,
    detail_entry_bias,
    detail_entry_kernel,
    detail_inner_scale,
    detail_inner_bias,
    detail_inner_kernel,
    detail_skip_projection,
):
    x = coarse.reshape(4, W, 512)
    stat = lambda c: shape(ROWS, 1, 2 * c, dtype=F32)
    parts, head, tail = call(
        coarse_stats_kernel, (stat(512), shape(2, W, 512), shape(2, W, 512)), name="coarse_stats"
    )(x)
    up = lax.ppermute(tail, "rows", [(i, (i + 1) % ROWS) for i in range(ROWS)])
    down = lax.ppermute(head, "rows", [((i + 1) % ROWS, i) for i in range(ROWS)])
    parts, gain, shift, packed = call(
        prepare_kernel_body,
        (stat(512), shape(1, 512, dtype=F32), shape(1, 512, dtype=F32), shape(2, 1024, 1024)),
        [pltpu.VMEM((3, 3, 512, 256), BF16), pltpu.SemaphoreType.DMA((5,))],
        name="prepare",
        flops=1 << 30,
        specs=[VMEM] + [HBM] * 3,
    )(parts, *(stay(v) for v in (line(broad_entry_scale), line(broad_entry_bias), broad_entry_kernel)))
    parts = swap(parts)
    wide_h, parts = call(
        broad_entry_kernel_body,
        (shape(12, W, 512), stat(256)),
        [pltpu.VMEM((8, W, 512), BF16)],
        name="broad_entry",
        flops=1 << 32,
    )(x, up, down, parts, gain, shift, packed)
    parts = swap(parts)
    wide_out, send, part = call(
        broad_inner_kernel_body,
        (shape(10, W, 512), shape(COLS, 184, 256), shape(1, 512, dtype=F32)),
        [
            pltpu.VMEM((12, W, 512), BF16),
            pltpu.VMEM((5, 2, W, 128), F32),
            pltpu.VMEM((5, 2, W + 8, 128), F32),
            pltpu.VMEM((2, COLS * 24, 128), F32),
        ],
        name="broad_inner",
        flops=1 << 32,
    )(
        wide_h,
        x,
        up,
        down,
        parts,
        line(broad_inner_scale),
        line(broad_inner_bias),
        broad_inner_kernel.reshape(9 * 256, 256),
        broad_skip_projection,
    )
    pair = jnp.concatenate([part, across_z(part)], axis=0)
    send, pair = lax.optimization_barrier((send, pair))
    blocks = lax.all_to_all(send, "cols", 0, 0, tiled=True)
    part, norm = call(
        detail_stats_kernel_body,
        (shape(1, 256, dtype=F32), shape(1, 512, dtype=F32)),
        [pltpu.VMEM((10, W, 512), BF16)] + [pltpu.VMEM((2, 2, 256, 256), BF16)] * 2,
        name="detail_stats",
        flops=1 << 32,
    )(wide_out, pair, *along_y(pair), line(detail_entry_scale), line(detail_entry_bias), detail_entry_kernel)
    here = jnp.concatenate([part] + along_y(part), axis=0)
    there = across_z(here)
    norms = call(summary_kernel_body, shape(COLS, 1, 768, dtype=F32), name="summary")(here, there, norm)
    blocks, norms = lax.optimization_barrier((blocks, norms))
    norms = lax.all_to_all(norms, "cols", 0, 0, tiled=True)
    blocks = jnp.transpose(blocks, (1, 0, 2))
    operands = (
        blocks,
        norms,
        line(detail_entry_scale),
        line(detail_entry_bias),
        line(detail_inner_scale),
        line(detail_inner_bias),
        detail_entry_kernel,
        detail_inner_kernel,
        detail_skip_projection,
    )
    return pl.pallas_call(
        detail_kernel_body,
        grid=(4,),
        in_specs=[pl.BlockSpec(v.shape, functools.partial(lambda n, i: (0,) * n, v.ndim)) for v in operands],
        out_specs=pl.BlockSpec((COLS, 4, 32, 128), lambda i: (0, i, 0, 0)),
        out_shape=shape(COLS, 16, 32, 128),
        scratch_shapes=[
            pltpu.VMEM((10, 18 * 16, 256), BF16),
            pltpu.VMEM((18, 17 * 16, 256), BF16),
            pltpu.VMEM((2, 2, 256, 256), BF16),
            pltpu.VMEM((2, 2, 256, 256), BF16),
            pltpu.VMEM((1536, 256), BF16),
            pltpu.VMEM((4, 512, 128), F32),
        ],
        name="detail",
        cost_estimate=pl.CostEstimate(flops=1 << 33, bytes_accessed=0, transcendentals=0),
        compiler_params=pltpu.CompilerParams(vmem_limit_bytes=VMEM_LIMIT),
    )(*operands)


def solution(mesh):
    return jax.shard_map(
        body,
        mesh=mesh,
        in_specs=(P("cols", "rows", None, None),) + (P(),) * 14,
        out_specs=P(None, "rows", "cols", None),
        check_vma=False,
    )
```

```python
import functools

import jax
import jax.numpy as jnp
from jax import lax
from jax.experimental import pallas as pl
from jax.experimental.pallas import tpu as pltpu
from jax.sharding import PartitionSpec as P

GROUPS = 32
EPSILON = 1e-06
F32 = jnp.float32
BF16 = jnp.bfloat16
ROWS = 8
COLS = 16
W = 128
VMEM_LIMIT = 24 * 1024 * 1024


VMEM = pl.BlockSpec(memory_space=pltpu.VMEM)
HBM = pl.BlockSpec(memory_space=pltpu.HBM)


def call(kernel, out_shape, scratch=(), flops=0, name=None, specs=None, outs=None):
    return pl.pallas_call(
        kernel,
        out_shape=out_shape,
        **({} if specs is None else {"in_specs": specs}),
        **({} if outs is None else {"out_specs": outs}),
        scratch_shapes=list(scratch),
        name=name,
        cost_estimate=pl.CostEstimate(flops=flops, bytes_accessed=0, transcendentals=0),
        compiler_params=pltpu.CompilerParams(vmem_limit_bytes=VMEM_LIMIT),
    )


def group_sum(v, size):
    count = v.shape[-1]
    lane = lax.broadcasted_iota(jnp.int32, v.shape, 1)
    step = 1
    while step < size:
        before = pltpu.roll(v, step, 1)
        after = pltpu.roll(v, count - step, 1)
        v = v + jnp.where((lane & step) != 0, before, after)
        step *= 2
    return v


def moments(parts, held):
    lines = []
    for ref in parts:
        lines += [ref[d] for d in range(ref.shape[0])] if len(ref.shape) == 3 else [ref[...]]
    both = jnp.concatenate(lines, axis=0)
    chans = both.shape[1] // 2
    size = chans // GROUPS
    sums, squares = both[:, :chans], both[:, chans:]
    entries = float(ROWS * held * size)
    total = jnp.broadcast_to(jnp.sum(sums, axis=0, keepdims=True), sums.shape)
    mean = group_sum(total, size) / entries
    off = sums / float(held) - mean
    spread = jnp.sum(squares + float(held) * off * off, axis=0, keepdims=True)
    spread = group_sum(jnp.broadcast_to(spread, sums.shape), size) / entries
    return mean, lax.rsqrt(spread + EPSILON)


def tile_lanes(v, times):
    return jnp.concatenate([v] * times, axis=1) if times > 1 else v


def active(value, mean, gain, shift):
    half = (value.astype(F32) - mean) * gain + shift
    return half + half * jnp.tanh(half)


def block_moments(blocks):
    sums, squares, sizes = [], [], []
    for block in blocks:
        n = block.shape[0]
        if n == 0:
            continue
        origin = jnp.mean(block[0:16], axis=0, keepdims=True)
        d = block - origin
        s = jnp.sum(d, axis=0, keepdims=True)
        q = jnp.sum(d * d, axis=0, keepdims=True)
        sums.append(s + float(n) * origin)
        squares.append(jnp.maximum(q - s * s / float(n), 0.0))
        sizes.append(n)
    total = functools.reduce(jnp.add, sums)
    mean = total / float(sum(sizes))
    out = functools.reduce(jnp.add, squares)
    for s, n in zip(sums, sizes):
        off = s / float(n) - mean
        out = out + float(n) * off * off
    return jnp.concatenate([total, out], axis=1)


def publish(ref, vector):
    for d in range(ROWS):
        ref[d] = vector


def next_col(v):
    col = lax.broadcasted_iota(jnp.int32, v.shape, 0) % W
    return jnp.where(col == W - 1, 0.0, pltpu.roll(v, v.shape[0] - 1, 0))


def last_col(v):
    col = lax.broadcasted_iota(jnp.int32, v.shape, 0) % W
    return jnp.where(col == 0, 0.0, pltpu.roll(v, 1, 0))


def edge_flags():
    row = lax.axis_index("rows")
    return row == 0, row == ROWS - 1


def mm(a, b):
    return jnp.dot(a, b, preferred_element_type=F32)


def coarse_stats_kernel(x_ref, out_ref, head_ref, tail_ref):
    x = x_ref[...].astype(F32).reshape(4 * W, 512)
    head_ref[...] = x_ref[0:2]
    tail_ref[...] = x_ref[2:4]
    publish(out_ref, block_moments([x]))


def pack_broad(k_ref, out_ref):
    rows = (((0,), (1, 2)), ((0, 1), (2,)))
    step = 128
    for a in range(2):
        for t in range(2):
            for c in range(0, 512, step):
                col = [
                    functools.reduce(
                        jnp.add, [k_ref[ky, kx, c : c + step, :].astype(F32) for ky in rows[a][t]]
                    )
                    for kx in range(3)
                ]
                for n, v in enumerate((col[0], col[1] + col[2], col[0] + col[1], col[2])):
                    out_ref[a, t * 512 + c : t * 512 + c + step, n * 256 : (n + 1) * 256] = v.astype(BF16)


def pack_detail(k_ref, x_ref, z_ref):
    rows = (((0,), (1, 2)), ((0, 1), (2,)))
    for a in range(2):
        for t in range(2):
            col = [
                functools.reduce(jnp.add, [k_ref[ky, kx].astype(F32) for ky in rows[a][t]])
                for kx in range(3)
            ]
            x_ref[a, t] = jnp.concatenate([col[0] + col[1], col[0]], axis=1).astype(BF16)
            z_ref[a, t] = jnp.concatenate([col[2], col[1] + col[2]], axis=1).astype(BF16)


def prepare_kernel_body(
    parts_ref, gain_hbm, shift_hbm, k_hbm, parts_out, gain_ref, shift_ref, w_ref, k_ref, sems
):
    pairs = ((gain_hbm, gain_ref), (shift_hbm, shift_ref)) + tuple((k_hbm.at[i], k_ref.at[i]) for i in range(3))
    copies = [pltpu.make_async_copy(src, dst, sems.at[i]) for i, (src, dst) in enumerate(pairs)]
    for copy in copies:
        copy.start()
    for d in range(ROWS):
        parts_out[d] = parts_ref[d]
    for copy in copies:
        copy.wait()
    pack_broad(k_ref, w_ref)


def broad_entry_kernel_body(
    x_ref, up_ref, down_ref, parts_ref, gain_ref, shift_ref, w_ref, out_ref, stat_ref, an
):
    first, last = edge_flags()
    mean, rate = moments([parts_ref], 4 * W)
    mean, gain, shift = mean[:1], 0.5 * rate[:1] * gain_ref[...], 0.5 * shift_ref[...]
    keep_up = jnp.where(first, 0.0, 1.0)
    keep_down = jnp.where(last, 0.0, 1.0)
    def norm(h):
        if h < 2:
            v = active(up_ref[h], mean, gain, shift) * keep_up
        elif h < 6:
            v = active(x_ref[h - 2], mean, gain, shift)
        else:
            v = active(down_ref[h - 6], mean, gain, shift) * keep_down
        an[h] = v.astype(BF16)

    ready, blocks, count = 0, [], 1
    for start in range(0, 6, count):
        while ready < start + count + 2:
            norm(ready)
            ready += 1
        lo, hi = max(start, 1) - start, min(start + count, 5) - start
        for a in range(2):
            near = an[start + a : start + a + count].reshape(count * W, 512)
            far = an[start + a + 1 : start + a + 1 + count].reshape(count * W, 512)
            both = jnp.concatenate([near, far], axis=1)
            for b in range(2):
                z = [mm(both, w_ref[a, :, n * 256 : (n + 1) * 256]) for n in (2 * b, 2 * b + 1)]
                v = last_col(z[0]) + z[1] if b == 0 else z[0] + next_col(z[1])
                for h in range(count):
                    out_ref[2 * (start + h) + a, :, b * 256 : (b + 1) * 256] = v[h * W : (h + 1) * W].astype(BF16)
                blocks.append(v[lo * W : hi * W])
    publish(stat_ref, block_moments(blocks))


def broad_inner_kernel_body(
    h_ref, x_ref, up_ref, down_ref, parts_ref, gain_ref, shift_ref, w_ref, p_ref,
    out_ref, send_hbm, stat_ref, an, odd_line, even_line, rim, send_ref, sems,
):
    first, last = edge_flags()
    mean, rate = moments([parts_ref], 8 * 2 * W)
    mean, gain, shift = mean[:1], 0.5 * rate[:1] * gain_ref[...], 0.5 * shift_ref[...]
    mean, gain, shift = (tile_lanes(v, 2) for v in (mean, gain, shift))
    keep_up = jnp.where(first, 0.0, 1.0)
    keep_down = jnp.where(last, 0.0, 1.0)
    def norm(i):
        v = active(h_ref[i], mean, gain, shift)
        if i < 2:
            v = v * keep_up
        elif i >= 10:
            v = v * keep_down
        an[i] = v.astype(BF16)

    skip_in = jnp.concatenate([up_ref[1]] + [x_ref[h] for h in range(4)] + [down_ref[0]], axis=0)
    skip = mm(skip_in, p_ref[...])
    w = w_ref
    even_w = jnp.concatenate([w[ky * 768 + 256 : ky * 768 + 768] for ky in range(3)], axis=0)
    odd_w = jnp.concatenate([w[ky * 768 : ky * 768 + 512] for ky in range(3)], axis=0)
    even_side = jnp.concatenate([w[ky * 768 : ky * 768 + 256] for ky in range(3)], axis=0)
    odd_side = jnp.concatenate([w[ky * 768 + 512 : ky * 768 + 768] for ky in range(3)], axis=0)
    copies = []

    def ship(at, size):
        rows = pl.ds(at, size)
        copies.append(pltpu.make_async_copy(send_ref.at[:, rows], send_hbm.at[:, rows], sems.at[len(copies)]))
        copies[-1].start()

    blocks, ready, count = [], 0, 2
    even_line[...] = jnp.zeros(even_line.shape, F32)
    rim[...] = jnp.zeros(rim.shape, F32)
    for j in range(0, 10, count):
        while ready < j + count + 2:
            norm(ready)
            ready += 1
        main = jnp.concatenate([an[j + ky : j + ky + count].reshape(count * W, 512) for ky in range(3)], axis=1)
        even_in = jnp.concatenate(
            [an[j + ky : j + ky + count, :, 0:256].reshape(count * W, 256) for ky in range(3)], axis=1
        )
        odd_in = jnp.concatenate(
            [an[j + ky : j + ky + count, :, 256:512].reshape(count * W, 256) for ky in range(3)], axis=1
        )
        extra = jnp.concatenate([skip[(i + 1) // 2 * W : ((i + 1) // 2 + 1) * W] for i in range(j, j + count)], axis=0)
        even = mm(main, even_w) + last_col(mm(odd_in, even_side)) + extra
        odd = mm(main, odd_w) + next_col(mm(even_in, odd_side)) + extra
        before = last_col(odd)
        for i in range(count):
            e, o, p = (v[i * W : (i + 1) * W] for v in (even, odd, before))
            out_ref[j + i, :, 0:256] = e.astype(BF16)
            out_ref[j + i, :, 256:512] = o.astype(BF16)
            block = jnp.concatenate([p.reshape(COLS, 8, 256), e.reshape(COLS, 8, 256)], axis=1)
            send_ref[:, (j + i) * 16 : (j + i + 1) * 16, :] = block.astype(BF16)
            for n in range(2):
                odd_line[i, n] = o[:, n * 128 : (n + 1) * 128]
                even_line[i, n, 0:W] = e[:, n * 128 : (n + 1) * 128]
                rim[n, pl.ds(j + i, COLS, stride=24), :] = odd_line[i, n, pl.ds(7, COLS, stride=8), :]
                rim[n, pl.ds(10 + j + i, COLS, stride=24), :] = even_line[i, n, pl.ds(8, COLS, stride=8), :]
        lo, hi = max(j, 1) - j, min(j + count, 9) - j
        blocks += [even[lo * W : hi * W], odd[lo * W : hi * W]]
        if j in (2, 6):
            ship((j - 2) * 16, 64)
    for n in range(2):
        send_ref[:, 160:184, n * 128 : (n + 1) * 128] = rim[n].reshape(COLS, 24, 128).astype(BF16)
    ship(128, 56)
    stat_ref[...] = block_moments(blocks)
    for copy in copies:
        copy.wait()


def detail_stats_kernel_body(
    x_ref, a_ref, b_ref, c_ref, d_ref, gain_ref, shift_ref, k_ref, stat_ref, norm_ref, an, wx_ref, wz_ref
):
    pack_detail(k_ref, wx_ref, wz_ref)
    first, last = edge_flags()
    mean, rate = moments([a_ref, b_ref, c_ref, d_ref], 8 * 2 * W)
    norm_ref[...] = jnp.concatenate([mean[:1], rate[:1]], axis=1)
    mean, gain, shift = mean[:1], 0.5 * rate[:1] * gain_ref[...], 0.5 * shift_ref[...]
    mean, gain, shift = (tile_lanes(v, 2) for v in (mean, gain, shift))
    keep_up = jnp.where(first, 0.0, 1.0)
    keep_down = jnp.where(last, 0.0, 1.0)
    for i in range(10):
        v = active(x_ref[i], mean, gain, shift)
        if i < 1:
            v = v * keep_up
        elif i >= 9:
            v = v * keep_down
        an[i] = v.astype(BF16)
    blocks = []
    for a in range(2):
        lhs = [an[a + t : a + t + 8].reshape(8 * W, 512) for t in range(2)]
        main = jnp.concatenate(lhs, axis=1)
        odd = jnp.concatenate([v[:, 256:512] for v in lhs], axis=1)
        even = jnp.concatenate([v[:, 0:256] for v in lhs], axis=1)
        wx = [wx_ref[a, t] for t in range(2)]
        wz = [wz_ref[a, t] for t in range(2)]
        middle = mm(main, jnp.concatenate([wx[0], wz[0], wx[1], wz[1]], axis=0))
        right = mm(odd, jnp.concatenate(wx, axis=0))
        left = mm(even, jnp.concatenate(wz, axis=0))
        q3 = right[:, 0:128] + next_col(left[:, 0:128])
        q0 = last_col(right[:, 128:256]) + left[:, 128:256]
        for v in (q3, q0, middle[:, 0:128], middle[:, 128:256]):
            blocks.append(v)
    stat_ref[...] = block_moments(blocks)


def summary_kernel_body(here_ref, there_ref, norm_ref, out_ref):
    mean, rate = moments([here_ref, there_ref], 16 * 4 * W)
    both = jnp.concatenate([mean[:1], rate[:1], norm_ref[...]], axis=1)
    for c in range(COLS):
        out_ref[c] = both


def pixel(j, u):
    if u == 15:
        return 160 + j
    if u == 16:
        return 170 + j
    return j * 16 + (8 + u // 2 if u % 2 == 0 else (u + 1) // 2)


PLAN = (('entry', 0, 3), ('entry', 3, 3), ('entry', 6, 3), ('inner', 0, 4), ('inner', 4, 4), ('send', 0, 8), ('inner', 8, 4), ('inner', 12, 4), ('send', 8, 8))


def detail_kernel_body(
    x_ref, norm_ref, gain3_ref, shift3_ref, gain4_ref, shift4_ref, k3_ref, k4_ref, p_ref,
    out_hbm, an3, an4, wx_ref, wz_ref, w_ref, tmp, out_ref, sems,
):
    pack_detail(k3_ref, wx_ref, wz_ref)
    zero = jnp.zeros((128, 128), BF16)
    for ky in range(3):
        k = [k4_ref[ky, kx] for kx in range(3)]
        table = ((k[0], zero), (k[1], k[0]), (k[2], k[1]), (zero, k[2]))
        for i, pair in enumerate(table):
            at = ky * 512 + i * 128
            w_ref[at : at + 128, 0:128] = pair[0]
            w_ref[at : at + 128, 128:256] = pair[1]
    first, last = edge_flags()
    keep_up = jnp.where(first, 0.0, 1.0)
    keep_down = jnp.where(last, 0.0, 1.0)
    col = lax.axis_index("cols")
    keep_left = jnp.where(col == 0, 0.0, 1.0)
    keep_right = jnp.where(col == COLS - 1, 0.0, 1.0)
    norm = jnp.concatenate([norm_ref[i] for i in range(COLS)], axis=0)
    mean4, rate4 = (tile_lanes(norm[:, n * 128 : (n + 1) * 128], 2) for n in range(2))
    mean3, rate3 = norm[:, 256:512], norm[:, 512:768]
    gain3, shift3 = 0.5 * rate3 * gain3_ref[...], 0.5 * shift3_ref[...]
    gain4, shift4 = 0.5 * rate4 * tile_lanes(gain4_ref[...], 2), 0.5 * tile_lanes(shift4_ref[...], 2)
    def norm3(j):
        for u in range(-1, 17):
            v = active(x_ref[pixel(j, u)], mean3, gain3, shift3)
            if j == 0:
                v = v * keep_up
            elif j == 9:
                v = v * keep_down
            if u == -1:
                v = v * keep_left
            elif u == 16:
                v = v * keep_right
            an3[j, (u + 1) * 16 : (u + 2) * 16] = v.astype(BF16)

    size = 17 * 16
    lane = lax.broadcasted_iota(jnp.int32, (16, 256), 1)
    left_mask = jnp.where(lane < 128, keep_left, 1.0)
    right_mask = jnp.where(lane >= 128, keep_right, 1.0)

    def entry(i, count):
        lhs = jnp.concatenate(
            [
                an3[i + t : i + t + count, s : s + size].reshape(count * size, 256)
                for t in range(2)
                for s in (0, 16)
            ],
            axis=1,
        )
        for a in range(2):
            w = jnp.concatenate([wx_ref[a, 0], wz_ref[a, 0], wx_ref[a, 1], wz_ref[a, 1]], axis=0)
            v = mm(lhs, w).astype(BF16).reshape(count * 17, 16, 256)
            v = active(v, mean4, gain4, shift4)
            for n in range(count):
                f = 2 * (i + n) + 1 - a
                line = v[n * 17 : (n + 1) * 17]
                if f == 0:
                    line = line * keep_up
                elif f == 17:
                    line = line * keep_down
                an4[f, 16 : size - 16] = line[1:16].reshape(15 * 16, 256).astype(BF16)
                an4[f, 0:16] = (line[0] * left_mask).astype(BF16)
                an4[f, size - 16 : size] = (line[16] * right_mask).astype(BF16)

    def inner(base, count):
        lhs = jnp.concatenate(
            [an4[base + ky : base + ky + count, s : s + 256].reshape(count * 256, 256) for ky in range(3) for s in (0, 16)],
            axis=1,
        )
        v = mm(lhs, w_ref[...])
        raw = [x_ref[pixel(j, u)] for j in range(base // 2 + 1, (base + count) // 2 + 1) for u in range(16)]
        skip = mm(jnp.concatenate(raw, axis=0), p_ref[...])
        for n in range(count):
            for b in range(2):
                part = v[n * 256 : (n + 1) * 256, b * 128 : (b + 1) * 128] + skip[n // 2 * 256 : (n // 2 + 1) * 256]
                for u in range(16):
                    at = (2 * u + b) * 16
                    tmp[n, at : at + 16] = part[u * 16 : (u + 1) * 16]
            for image in range(16):
                out_ref[image, base + n] = tmp[n, pl.ds(image, 32, stride=16), :].astype(BF16)

    copies = []

    def send(base, count):
        rows = pl.ds(base, count)
        copies.append(pltpu.make_async_copy(out_ref.at[:, rows], out_hbm.at[:, rows], sems.at[len(copies)]))
        copies[-1].start()

    ready = 0
    for kind, base, count in PLAN:
        if kind == "entry":
            while ready < base + count + 1:
                norm3(ready)
                ready += 1
            entry(base, count)
        elif kind == "inner":
            inner(base, count)
        else:
            send(base, count)
    for copy in copies:
        copy.wait()


def swap(parts):
    return lax.all_to_all(parts, "rows", 0, 0, tiled=True)


def across_z(v):
    return lax.ppermute(v, "rows", [(i, i ^ 1) for i in range(ROWS)])


def along_y(v):
    return [lax.ppermute(v, "rows", [(i, (i + 2 * k) % ROWS) for i in range(ROWS)]) for k in range(1, 4)]


def shape(*dims, dtype=BF16):
    return jax.ShapeDtypeStruct(dims, dtype)


def stay(v):
    return pltpu.with_memory_space_constraint(v, pltpu.HBM)


def line(v):
    return v.reshape(1, -1)


def detail_call(*operands):
    return pl.pallas_call(
        detail_kernel_body,
        in_specs=[VMEM] * len(operands),
        out_specs=HBM,
        out_shape=shape(COLS, 16, 32, 128),
        scratch_shapes=[
            pltpu.VMEM((10, 18 * 16, 256), BF16),
            pltpu.VMEM((18, 17 * 16, 256), BF16),
            pltpu.VMEM((2, 2, 256, 256), BF16),
            pltpu.VMEM((2, 2, 256, 256), BF16),
            pltpu.VMEM((1536, 256), BF16),
            pltpu.VMEM((8, 512, 128), F32),
            pltpu.VMEM((COLS, 16, 32, 128), BF16),
            pltpu.SemaphoreType.DMA((6,)),
        ],
        name="detail",
        cost_estimate=pl.CostEstimate(flops=1 << 33, bytes_accessed=0, transcendentals=0),
        compiler_params=pltpu.CompilerParams(vmem_limit_bytes=VMEM_LIMIT),
    )(*operands)


def body(
    coarse,
    broad_entry_scale,
    broad_entry_bias,
    broad_entry_kernel,
    broad_inner_scale,
    broad_inner_bias,
    broad_inner_kernel,
    broad_skip_projection,
    detail_entry_scale,
    detail_entry_bias,
    detail_entry_kernel,
    detail_inner_scale,
    detail_inner_bias,
    detail_inner_kernel,
    detail_skip_projection,
):
    x = coarse.reshape(4, W, 512)
    stat = lambda c: shape(ROWS, 1, 2 * c, dtype=F32)
    parts, head, tail = call(
        coarse_stats_kernel, (stat(512), shape(2, W, 512), shape(2, W, 512)), name="coarse_stats"
    )(x)
    up = lax.ppermute(tail, "rows", [(i, (i + 1) % ROWS) for i in range(ROWS)])
    down = lax.ppermute(head, "rows", [((i + 1) % ROWS, i) for i in range(ROWS)])
    parts, gain, shift, packed = call(
        prepare_kernel_body,
        (stat(512), shape(1, 512, dtype=F32), shape(1, 512, dtype=F32), shape(2, 1024, 1024)),
        [pltpu.VMEM((3, 3, 512, 256), BF16), pltpu.SemaphoreType.DMA((5,))],
        name="prepare",
        flops=1 << 30,
        specs=[VMEM] + [HBM] * 3,
    )(parts, *(stay(v) for v in (line(broad_entry_scale), line(broad_entry_bias), broad_entry_kernel)))
    parts = swap(parts)
    wide_h, parts = call(
        broad_entry_kernel_body,
        (shape(12, W, 512), stat(256)),
        [pltpu.VMEM((8, W, 512), BF16)],
        name="broad_entry",
        flops=1 << 32,
    )(x, up, down, parts, gain, shift, packed)
    parts = swap(parts)
    wide_out, send, part = call(
        broad_inner_kernel_body,
        (shape(10, W, 512), shape(COLS, 184, 256), shape(1, 512, dtype=F32)),
        [
            pltpu.VMEM((12, W, 512), BF16),
            pltpu.VMEM((5, 2, W, 128), F32),
            pltpu.VMEM((5, 2, W + 8, 128), F32),
            pltpu.VMEM((2, COLS * 24, 128), F32),
            pltpu.VMEM((COLS, 184, 256), BF16),
            pltpu.SemaphoreType.DMA((3,)),
        ],
        name="broad_inner",
        flops=1 << 32,
        outs=(VMEM, HBM, VMEM),
    )(
        wide_h,
        x,
        up,
        down,
        parts,
        line(broad_inner_scale),
        line(broad_inner_bias),
        broad_inner_kernel.reshape(9 * 256, 256),
        broad_skip_projection,
    )
    pair = jnp.concatenate([part, across_z(part)], axis=0)
    send, pair = lax.optimization_barrier((send, pair))
    blocks = lax.all_to_all(send, "cols", 0, 0, tiled=True)
    part, norm = call(
        detail_stats_kernel_body,
        (shape(1, 256, dtype=F32), shape(1, 512, dtype=F32)),
        [pltpu.VMEM((10, W, 512), BF16)] + [pltpu.VMEM((2, 2, 256, 256), BF16)] * 2,
        name="detail_stats",
        flops=1 << 32,
    )(wide_out, pair, *along_y(pair), line(detail_entry_scale), line(detail_entry_bias), detail_entry_kernel)
    here = jnp.concatenate([part] + along_y(part), axis=0)
    there = across_z(here)
    norms = call(summary_kernel_body, shape(COLS, 1, 768, dtype=F32), name="summary")(here, there, norm)
    blocks, norms = lax.optimization_barrier((blocks, norms))
    norms = lax.all_to_all(norms, "cols", 0, 0, tiled=True)
    blocks = jnp.transpose(blocks, (1, 0, 2))
    return detail_call(
        blocks,
        norms,
        line(detail_entry_scale),
        line(detail_entry_bias),
        line(detail_inner_scale),
        line(detail_inner_bias),
        detail_entry_kernel,
        detail_inner_kernel,
        detail_skip_projection,
    )


def solution(mesh):
    return jax.shard_map(
        body,
        mesh=mesh,
        in_specs=(P("cols", "rows", None, None),) + (P(),) * 14,
        out_specs=P(None, "rows", "cols", None),
        check_vma=False,
    )
```

```python
import functools

import jax
import jax.numpy as jnp
from jax import lax
from jax.experimental import pallas as pl
from jax.experimental.pallas import tpu as pltpu
from jax.sharding import PartitionSpec as P

GROUPS = 32
EPSILON = 1e-06
F32 = jnp.float32
BF16 = jnp.bfloat16
ROWS = 8
COLS = 16
W = 128
VMEM_LIMIT = 24 * 1024 * 1024


VMEM = pl.BlockSpec(memory_space=pltpu.VMEM)
HBM = pl.BlockSpec(memory_space=pltpu.HBM)


def call(kernel, out_shape, scratch=(), flops=0, name=None, specs=None, outs=None):
    return pl.pallas_call(
        kernel,
        out_shape=out_shape,
        **({} if specs is None else {"in_specs": specs}),
        **({} if outs is None else {"out_specs": outs}),
        scratch_shapes=list(scratch),
        name=name,
        cost_estimate=pl.CostEstimate(flops=flops, bytes_accessed=0, transcendentals=0),
        compiler_params=pltpu.CompilerParams(vmem_limit_bytes=VMEM_LIMIT),
    )


def group_sum(v, size):
    count = v.shape[-1]
    lane = lax.broadcasted_iota(jnp.int32, v.shape, 1)
    step = 1
    while step < size:
        before = pltpu.roll(v, step, 1)
        after = pltpu.roll(v, count - step, 1)
        v = v + jnp.where((lane & step) != 0, before, after)
        step *= 2
    return v


def moments(parts, held):
    lines = []
    for ref in parts:
        lines += [ref[d] for d in range(ref.shape[0])] if len(ref.shape) == 3 else [ref[...]]
    both = jnp.concatenate(lines, axis=0)
    chans = both.shape[1] // 2
    size = chans // GROUPS
    sums, squares = both[:, :chans], both[:, chans:]
    entries = float(ROWS * held * size)
    total = jnp.broadcast_to(jnp.sum(sums, axis=0, keepdims=True), sums.shape)
    mean = group_sum(total, size) / entries
    off = sums / float(held) - mean
    spread = jnp.sum(squares + float(held) * off * off, axis=0, keepdims=True)
    spread = group_sum(jnp.broadcast_to(spread, sums.shape), size) / entries
    return mean, lax.rsqrt(spread + EPSILON)


def tile_lanes(v, times):
    return jnp.concatenate([v] * times, axis=1) if times > 1 else v


def active(value, mean, gain, shift):
    half = (value.astype(F32) - mean) * gain + shift
    return half + half * jnp.tanh(half)


def piece(block):
    n = block.shape[0]
    origin = jnp.mean(block[0:16], axis=0, keepdims=True)
    d = block - origin
    s = jnp.sum(d, axis=0, keepdims=True)
    q = jnp.sum(d * d, axis=0, keepdims=True)
    return n, s + float(n) * origin, jnp.maximum(q - s * s / float(n), 0.0)


def merge(pieces):
    total = functools.reduce(jnp.add, [s for _, s, _ in pieces])
    mean = total / float(sum(n for n, _, _ in pieces))
    out = functools.reduce(jnp.add, [q for _, _, q in pieces])
    for n, s, _ in pieces:
        off = s / float(n) - mean
        out = out + float(n) * off * off
    return jnp.concatenate([total, out], axis=1)


def publish(ref, vector):
    for d in range(ROWS):
        ref[d] = vector


def next_col(v):
    col = lax.broadcasted_iota(jnp.int32, v.shape, 0) % W
    return jnp.where(col == W - 1, 0.0, pltpu.roll(v, v.shape[0] - 1, 0))


def last_col(v):
    col = lax.broadcasted_iota(jnp.int32, v.shape, 0) % W
    return jnp.where(col == 0, 0.0, pltpu.roll(v, 1, 0))


def edge_flags():
    row = lax.axis_index("rows")
    return row == 0, row == ROWS - 1


def mm(a, b):
    return jnp.dot(a, b, preferred_element_type=F32)


def coarse_stats_kernel(x_ref, out_ref, head_ref, tail_ref):
    x = x_ref[...].astype(F32).reshape(4 * W, 512)
    head_ref[...] = x_ref[0:2]
    tail_ref[...] = x_ref[2:4]
    publish(out_ref, merge([piece(x)]))


def pack_broad(k_ref, out_ref):
    rows = (((0,), (1, 2)), ((0, 1), (2,)))
    step = 128
    for a in range(2):
        for t in range(2):
            for c in range(0, 512, step):
                col = [
                    functools.reduce(
                        jnp.add, [k_ref[ky, kx, c : c + step, :].astype(F32) for ky in rows[a][t]]
                    )
                    for kx in range(3)
                ]
                for n, v in enumerate((col[0], col[1] + col[2], col[0] + col[1], col[2])):
                    out_ref[a, t * 512 + c : t * 512 + c + step, n * 256 : (n + 1) * 256] = v.astype(BF16)


def pack_detail(k_ref, x_ref, z_ref):
    rows = (((0,), (1, 2)), ((0, 1), (2,)))
    for a in range(2):
        for t in range(2):
            col = [
                functools.reduce(jnp.add, [k_ref[ky, kx].astype(F32) for ky in rows[a][t]])
                for kx in range(3)
            ]
            x_ref[a, t] = jnp.concatenate([col[0] + col[1], col[0]], axis=1).astype(BF16)
            z_ref[a, t] = jnp.concatenate([col[2], col[1] + col[2]], axis=1).astype(BF16)


def prepare_kernel_body(
    parts_ref, gain_hbm, shift_hbm, k_hbm, parts_out, gain_ref, shift_ref, w_ref, k_ref, sems
):
    pairs = ((gain_hbm, gain_ref), (shift_hbm, shift_ref)) + tuple((k_hbm.at[i], k_ref.at[i]) for i in range(3))
    copies = [pltpu.make_async_copy(src, dst, sems.at[i]) for i, (src, dst) in enumerate(pairs)]
    for copy in copies:
        copy.start()
    for d in range(ROWS):
        parts_out[d] = parts_ref[d]
    for copy in copies:
        copy.wait()
    pack_broad(k_ref, w_ref)


def broad_entry_kernel_body(
    x_ref, up_ref, down_ref, parts_ref, gain_ref, shift_ref, w_ref, out_ref, stat_ref, an
):
    first, last = edge_flags()
    mean, rate = moments([parts_ref], 4 * W)
    mean, gain, shift = mean[:1], 0.5 * rate[:1] * gain_ref[...], 0.5 * shift_ref[...]
    keep_up = jnp.where(first, 0.0, 1.0)
    keep_down = jnp.where(last, 0.0, 1.0)
    def norm(h):
        if h < 2:
            v = active(up_ref[h], mean, gain, shift) * keep_up
        elif h < 6:
            v = active(x_ref[h - 2], mean, gain, shift)
        else:
            v = active(down_ref[h - 6], mean, gain, shift) * keep_down
        an[h] = v.astype(BF16)

    ready, pieces, count = 0, [], 1
    for start in range(0, 6, count):
        while ready < start + count + 2:
            norm(ready)
            ready += 1
        lo, hi = max(start, 1) - start, min(start + count, 5) - start
        for a in range(2):
            near = an[start + a : start + a + count].reshape(count * W, 512)
            far = an[start + a + 1 : start + a + 1 + count].reshape(count * W, 512)
            both = jnp.concatenate([near, far], axis=1)
            for b in range(2):
                z = mm(both, w_ref[a, :, b * 512 : (b + 1) * 512])
                z = [z[:, 0:256], z[:, 256:512]]
                v = last_col(z[0]) + z[1] if b == 0 else z[0] + next_col(z[1])
                for h in range(count):
                    out_ref[2 * (start + h) + a, :, b * 256 : (b + 1) * 256] = v[h * W : (h + 1) * W].astype(BF16)
                if lo < hi:
                    pieces.append(piece(v[lo * W : hi * W]))
    publish(stat_ref, merge(pieces))


def broad_inner_kernel_body(
    h_ref, x_ref, up_ref, down_ref, parts_ref, gain_ref, shift_ref, w_ref, p_ref,
    out_ref, stat_ref, an,
):
    first, last = edge_flags()
    mean, rate = moments([parts_ref], 8 * 2 * W)
    mean, gain, shift = mean[:1], 0.5 * rate[:1] * gain_ref[...], 0.5 * shift_ref[...]
    mean, gain, shift = (tile_lanes(v, 2) for v in (mean, gain, shift))
    keep_up = jnp.where(first, 0.0, 1.0)
    keep_down = jnp.where(last, 0.0, 1.0)
    def norm(i):
        v = active(h_ref[i], mean, gain, shift)
        if i < 2:
            v = v * keep_up
        elif i >= 10:
            v = v * keep_down
        an[i] = v.astype(BF16)

    skip_in = jnp.concatenate([up_ref[1]] + [x_ref[h] for h in range(4)] + [down_ref[0]], axis=0)
    skip = mm(skip_in, p_ref[...])
    w = w_ref
    even_w = jnp.concatenate([w[ky * 768 + 256 : ky * 768 + 768] for ky in range(3)], axis=0)
    odd_w = jnp.concatenate([w[ky * 768 : ky * 768 + 512] for ky in range(3)], axis=0)
    even_side = jnp.concatenate([w[ky * 768 : ky * 768 + 256] for ky in range(3)], axis=0)
    odd_side = jnp.concatenate([w[ky * 768 + 512 : ky * 768 + 768] for ky in range(3)], axis=0)
    pieces, ready, count = [], 0, 2
    for j in range(0, 10, count):
        while ready < j + count + 2:
            norm(ready)
            ready += 1
        main = jnp.concatenate([an[j + ky : j + ky + count].reshape(count * W, 512) for ky in range(3)], axis=1)
        even_in = jnp.concatenate(
            [an[j + ky : j + ky + count, :, 0:256].reshape(count * W, 256) for ky in range(3)], axis=1
        )
        odd_in = jnp.concatenate(
            [an[j + ky : j + ky + count, :, 256:512].reshape(count * W, 256) for ky in range(3)], axis=1
        )
        extra = jnp.concatenate([skip[(i + 1) // 2 * W : ((i + 1) // 2 + 1) * W] for i in range(j, j + count)], axis=0)
        even = mm(main, even_w) + last_col(mm(odd_in, even_side)) + extra
        odd = mm(main, odd_w) + next_col(mm(even_in, odd_side)) + extra
        for i in range(count):
            out_ref[j + i, :, 0:256] = even[i * W : (i + 1) * W].astype(BF16)
            out_ref[j + i, :, 256:512] = odd[i * W : (i + 1) * W].astype(BF16)
        lo, hi = max(j, 1) - j, min(j + count, 9) - j
        pieces += [piece(v[lo * W : hi * W]) for v in (even, odd)]
    stat_ref[...] = merge(pieces)


def arrange_kernel_body(x_ref, send_hbm, odd_line, even_line, rim, send_ref, sems):
    copies = []

    def ship(at, size):
        rows = pl.ds(at, size)
        copies.append(pltpu.make_async_copy(send_ref.at[:, rows], send_hbm.at[:, rows], sems.at[len(copies)]))
        copies[-1].start()

    even_line[...] = jnp.zeros(even_line.shape, F32)
    rim[...] = jnp.zeros(rim.shape, F32)
    for j in range(10):
        e, o = x_ref[j, :, 0:256].astype(F32), x_ref[j, :, 256:512].astype(F32)
        block = jnp.concatenate([last_col(o).reshape(COLS, 8, 256), e.reshape(COLS, 8, 256)], axis=1)
        send_ref[:, j * 16 : (j + 1) * 16, :] = block.astype(BF16)
        for n in range(2):
            odd_line[j, n] = o[:, n * 128 : (n + 1) * 128]
            even_line[j, n, 0:W] = e[:, n * 128 : (n + 1) * 128]
            rim[n, pl.ds(j, COLS, stride=24), :] = odd_line[j, n, pl.ds(7, COLS, stride=8), :]
            rim[n, pl.ds(10 + j, COLS, stride=24), :] = even_line[j, n, pl.ds(8, COLS, stride=8), :]
        if j in (3, 7):
            ship((j - 3) * 16, 64)
    for n in range(2):
        send_ref[:, 160:184, n * 128 : (n + 1) * 128] = rim[n].reshape(COLS, 24, 128).astype(BF16)
    ship(128, 56)
    for copy in copies:
        copy.wait()


def detail_stats_kernel_body(
    x_ref, a_ref, b_ref, c_ref, d_ref, gain_ref, shift_ref, k_ref, stat_ref, norm_ref, an, wx_ref, wz_ref
):
    pack_detail(k_ref, wx_ref, wz_ref)
    first, last = edge_flags()
    mean, rate = moments([a_ref, b_ref, c_ref, d_ref], 8 * 2 * W)
    norm_ref[...] = jnp.concatenate([mean[:1], rate[:1]], axis=1)
    mean, gain, shift = mean[:1], 0.5 * rate[:1] * gain_ref[...], 0.5 * shift_ref[...]
    mean, gain, shift = (tile_lanes(v, 2) for v in (mean, gain, shift))
    keep_up = jnp.where(first, 0.0, 1.0)
    keep_down = jnp.where(last, 0.0, 1.0)
    def norm(i):
        v = active(x_ref[i], mean, gain, shift)
        if i < 1:
            v = v * keep_up
        elif i >= 9:
            v = v * keep_down
        an[i] = v.astype(BF16)

    pieces, ready, count = [], 0, 4
    for start in range(0, 9 - count, count):
        while ready < start + count + 2:
            norm(ready)
            ready += 1
        for a in range(2):
            lhs = [an[start + a + t : start + a + t + count].reshape(count * W, 512) for t in range(2)]
            main = jnp.concatenate(lhs, axis=1)
            odd = jnp.concatenate([v[:, 256:512] for v in lhs], axis=1)
            even = jnp.concatenate([v[:, 0:256] for v in lhs], axis=1)
            wx = [wx_ref[a, t] for t in range(2)]
            wz = [wz_ref[a, t] for t in range(2)]
            middle = mm(main, jnp.concatenate([wx[0], wz[0], wx[1], wz[1]], axis=0))
            right = mm(odd, jnp.concatenate(wx, axis=0))
            left = mm(even, jnp.concatenate(wz, axis=0))
            q3 = right[:, 0:128] + next_col(left[:, 0:128])
            q0 = last_col(right[:, 128:256]) + left[:, 128:256]
            pieces += [piece(v) for v in (q3, q0, middle[:, 0:128], middle[:, 128:256])]
    stat_ref[...] = merge(pieces)


def summary_kernel_body(here_ref, there_ref, norm_ref, out_ref):
    mean, rate = moments([here_ref, there_ref], 16 * 4 * W)
    both = jnp.concatenate([mean[:1], rate[:1], norm_ref[...]], axis=1)
    for c in range(COLS):
        out_ref[c] = both


def pixel(j, u):
    if u == 15:
        return 160 + j
    if u == 16:
        return 170 + j
    return j * 16 + (8 + u // 2 if u % 2 == 0 else (u + 1) // 2)


PLAN = (('entry', 0, 3), ('entry', 3, 3), ('entry', 6, 3), ('inner', 0, 4), ('inner', 4, 4), ('send', 0, 8), ('inner', 8, 4), ('inner', 12, 4), ('send', 8, 8))


def detail_kernel_body(
    x_ref, norm_ref, gain3_ref, shift3_ref, gain4_ref, shift4_ref, k3_ref, k4_ref, p_ref,
    out_hbm, an3, an4, wx_ref, wz_ref, w_ref, tmp, out_ref, sems,
):
    pack_detail(k3_ref, wx_ref, wz_ref)
    zero = jnp.zeros((128, 128), BF16)
    for ky in range(3):
        k = [k4_ref[ky, kx] for kx in range(3)]
        table = ((k[0], zero), (k[1], k[0]), (k[2], k[1]), (zero, k[2]))
        for i, pair in enumerate(table):
            at = ky * 512 + i * 128
            w_ref[at : at + 128, 0:128] = pair[0]
            w_ref[at : at + 128, 128:256] = pair[1]
    first, last = edge_flags()
    keep_up = jnp.where(first, 0.0, 1.0)
    keep_down = jnp.where(last, 0.0, 1.0)
    col = lax.axis_index("cols")
    keep_left = jnp.where(col == 0, 0.0, 1.0)
    keep_right = jnp.where(col == COLS - 1, 0.0, 1.0)
    norm = jnp.concatenate([norm_ref[i] for i in range(COLS)], axis=0)
    mean4, rate4 = (tile_lanes(norm[:, n * 128 : (n + 1) * 128], 2) for n in range(2))
    mean3, rate3 = norm[:, 256:512], norm[:, 512:768]
    gain3, shift3 = 0.5 * rate3 * gain3_ref[...], 0.5 * shift3_ref[...]
    gain4, shift4 = 0.5 * rate4 * tile_lanes(gain4_ref[...], 2), 0.5 * tile_lanes(shift4_ref[...], 2)
    def norm3(j):
        for u in range(-1, 17):
            v = active(x_ref[pixel(j, u)], mean3, gain3, shift3)
            if j == 0:
                v = v * keep_up
            elif j == 9:
                v = v * keep_down
            if u == -1:
                v = v * keep_left
            elif u == 16:
                v = v * keep_right
            an3[j, (u + 1) * 16 : (u + 2) * 16] = v.astype(BF16)

    size = 17 * 16
    lane = lax.broadcasted_iota(jnp.int32, (16, 256), 1)
    left_mask = jnp.where(lane < 128, keep_left, 1.0)
    right_mask = jnp.where(lane >= 128, keep_right, 1.0)

    def entry(i, count):
        lhs = jnp.concatenate(
            [
                an3[i + t : i + t + count, s : s + size].reshape(count * size, 256)
                for t in range(2)
                for s in (0, 16)
            ],
            axis=1,
        )
        w = [jnp.concatenate([wx_ref[a, 0], wz_ref[a, 0], wx_ref[a, 1], wz_ref[a, 1]], axis=0) for a in range(2)]
        both = mm(lhs, jnp.concatenate(w, axis=1))
        for a in range(2):
            v = both[:, a * 256 : (a + 1) * 256].astype(BF16).reshape(count * 17, 16, 256)
            v = active(v, mean4, gain4, shift4)
            for n in range(count):
                f = 2 * (i + n) + 1 - a
                line = v[n * 17 : (n + 1) * 17]
                if f == 0:
                    line = line * keep_up
                elif f == 17:
                    line = line * keep_down
                an4[f, 16 : size - 16] = line[1:16].reshape(15 * 16, 256).astype(BF16)
                an4[f, 0:16] = (line[0] * left_mask).astype(BF16)
                an4[f, size - 16 : size] = (line[16] * right_mask).astype(BF16)

    def inner(base, count):
        lhs = jnp.concatenate(
            [an4[base + ky : base + ky + count, s : s + 256].reshape(count * 256, 256) for ky in range(3) for s in (0, 16)],
            axis=1,
        )
        v = mm(lhs, w_ref[...])
        raw = [x_ref[pixel(j, u)] for j in range(base // 2 + 1, (base + count) // 2 + 1) for u in range(16)]
        skip = mm(jnp.concatenate(raw, axis=0), p_ref[...])
        for n in range(count):
            for b in range(2):
                part = v[n * 256 : (n + 1) * 256, b * 128 : (b + 1) * 128] + skip[n // 2 * 256 : (n // 2 + 1) * 256]
                for u in range(16):
                    at = (2 * u + b) * 16
                    tmp[n, at : at + 16] = part[u * 16 : (u + 1) * 16]
            for image in range(16):
                out_ref[image, base + n] = tmp[n, pl.ds(image, 32, stride=16), :].astype(BF16)

    copies = []

    def send(base, count):
        rows = pl.ds(base, count)
        copies.append(pltpu.make_async_copy(out_ref.at[:, rows], out_hbm.at[:, rows], sems.at[len(copies)]))
        copies[-1].start()

    ready = 0
    for kind, base, count in PLAN:
        if kind == "entry":
            while ready < base + count + 1:
                norm3(ready)
                ready += 1
            entry(base, count)
        elif kind == "inner":
            inner(base, count)
        else:
            send(base, count)
    for copy in copies:
        copy.wait()


def swap(parts):
    return lax.all_to_all(parts, "rows", 0, 0, tiled=True)


def across_z(v):
    return lax.ppermute(v, "rows", [(i, i ^ 1) for i in range(ROWS)])


def along_y(v):
    return [lax.ppermute(v, "rows", [(i, (i + 2 * k) % ROWS) for i in range(ROWS)]) for k in range(1, 4)]


def shape(*dims, dtype=BF16):
    return jax.ShapeDtypeStruct(dims, dtype)


def stay(v):
    return pltpu.with_memory_space_constraint(v, pltpu.HBM)


def line(v):
    return v.reshape(1, -1)


def detail_call(*operands):
    return pl.pallas_call(
        detail_kernel_body,
        in_specs=[VMEM] * len(operands),
        out_specs=HBM,
        out_shape=shape(COLS, 16, 32, 128),
        scratch_shapes=[
            pltpu.VMEM((10, 18 * 16, 256), BF16),
            pltpu.VMEM((18, 17 * 16, 256), BF16),
            pltpu.VMEM((2, 2, 256, 256), BF16),
            pltpu.VMEM((2, 2, 256, 256), BF16),
            pltpu.VMEM((1536, 256), BF16),
            pltpu.VMEM((8, 512, 128), F32),
            pltpu.VMEM((COLS, 16, 32, 128), BF16),
            pltpu.SemaphoreType.DMA((6,)),
        ],
        name="detail",
        cost_estimate=pl.CostEstimate(flops=1 << 33, bytes_accessed=0, transcendentals=0),
        compiler_params=pltpu.CompilerParams(vmem_limit_bytes=VMEM_LIMIT),
    )(*operands)


def body(
    coarse,
    broad_entry_scale,
    broad_entry_bias,
    broad_entry_kernel,
    broad_inner_scale,
    broad_inner_bias,
    broad_inner_kernel,
    broad_skip_projection,
    detail_entry_scale,
    detail_entry_bias,
    detail_entry_kernel,
    detail_inner_scale,
    detail_inner_bias,
    detail_inner_kernel,
    detail_skip_projection,
):
    x = coarse.reshape(4, W, 512)
    stat = lambda c: shape(ROWS, 1, 2 * c, dtype=F32)
    parts, head, tail = call(
        coarse_stats_kernel, (stat(512), shape(2, W, 512), shape(2, W, 512)), name="coarse_stats"
    )(x)
    up = lax.ppermute(tail, "rows", [(i, (i + 1) % ROWS) for i in range(ROWS)])
    down = lax.ppermute(head, "rows", [((i + 1) % ROWS, i) for i in range(ROWS)])
    parts, gain, shift, packed = call(
        prepare_kernel_body,
        (stat(512), shape(1, 512, dtype=F32), shape(1, 512, dtype=F32), shape(2, 1024, 1024)),
        [pltpu.VMEM((3, 3, 512, 256), BF16), pltpu.SemaphoreType.DMA((5,))],
        name="prepare",
        flops=1 << 30,
        specs=[VMEM] + [HBM] * 3,
    )(parts, *(stay(v) for v in (line(broad_entry_scale), line(broad_entry_bias), broad_entry_kernel)))
    parts = swap(parts)
    wide_h, parts = call(
        broad_entry_kernel_body,
        (shape(12, W, 512), stat(256)),
        [pltpu.VMEM((8, W, 512), BF16)],
        name="broad_entry",
        flops=1 << 32,
    )(x, up, down, parts, gain, shift, packed)
    parts = swap(parts)
    wide_out, part = call(
        broad_inner_kernel_body,
        (shape(10, W, 512), shape(1, 512, dtype=F32)),
        [pltpu.VMEM((12, W, 512), BF16)],
        name="broad_inner",
        flops=1 << 32,
    )(
        wide_h,
        x,
        up,
        down,
        parts,
        line(broad_inner_scale),
        line(broad_inner_bias),
        broad_inner_kernel.reshape(9 * 256, 256),
        broad_skip_projection,
    )
    send = call(
        arrange_kernel_body,
        shape(COLS, 184, 256),
        [
            pltpu.VMEM((10, 2, W, 128), F32),
            pltpu.VMEM((10, 2, W + 8, 128), F32),
            pltpu.VMEM((2, COLS * 24, 128), F32),
            pltpu.VMEM((COLS, 184, 256), BF16),
            pltpu.SemaphoreType.DMA((3,)),
        ],
        name="arrange",
        flops=1 << 30,
        outs=HBM,
    )(wide_out)
    pair = jnp.concatenate([part, across_z(part)], axis=0)
    send, pair = lax.optimization_barrier((send, pair))
    blocks = lax.all_to_all(send, "cols", 0, 0, tiled=True)
    part, norm = call(
        detail_stats_kernel_body,
        (shape(1, 256, dtype=F32), shape(1, 512, dtype=F32)),
        [pltpu.VMEM((10, W, 512), BF16)] + [pltpu.VMEM((2, 2, 256, 256), BF16)] * 2,
        name="detail_stats",
        flops=1 << 32,
    )(wide_out, pair, *along_y(pair), line(detail_entry_scale), line(detail_entry_bias), detail_entry_kernel)
    here = jnp.concatenate([part] + along_y(part), axis=0)
    there = across_z(here)
    norms = call(summary_kernel_body, shape(COLS, 1, 768, dtype=F32), name="summary")(here, there, norm)
    blocks, norms = lax.optimization_barrier((blocks, norms))
    norms = lax.all_to_all(norms, "cols", 0, 0, tiled=True)
    blocks = jnp.transpose(blocks, (1, 0, 2))
    return detail_call(
        blocks,
        norms,
        line(detail_entry_scale),
        line(detail_entry_bias),
        line(detail_inner_scale),
        line(detail_inner_bias),
        detail_entry_kernel,
        detail_inner_kernel,
        detail_skip_projection,
    )


def solution(mesh):
    return jax.shard_map(
        body,
        mesh=mesh,
        in_specs=(P("cols", "rows", None, None),) + (P(),) * 14,
        out_specs=P(None, "rows", "cols", None),
        check_vma=False,
    )
```

```python
import functools

import jax
import jax.numpy as jnp
from jax import lax
from jax.experimental import pallas as pl
from jax.experimental.pallas import tpu as pltpu
from jax.sharding import PartitionSpec as P

GROUPS = 32
EPSILON = 1e-06
F32 = jnp.float32
BF16 = jnp.bfloat16
ROWS = 8
COLS = 16
W = 128
VMEM_LIMIT = 24 * 1024 * 1024


VMEM = pl.BlockSpec(memory_space=pltpu.VMEM)
HBM = pl.BlockSpec(memory_space=pltpu.HBM)


def call(kernel, out_shape, scratch=(), flops=0, name=None, specs=None, outs=None):
    return pl.pallas_call(
        kernel,
        out_shape=out_shape,
        **({} if specs is None else {"in_specs": specs}),
        **({} if outs is None else {"out_specs": outs}),
        scratch_shapes=list(scratch),
        name=name,
        cost_estimate=pl.CostEstimate(flops=flops, bytes_accessed=0, transcendentals=0),
        compiler_params=pltpu.CompilerParams(vmem_limit_bytes=VMEM_LIMIT),
    )


def group_sum(v, size):
    count = v.shape[-1]
    lane = lax.broadcasted_iota(jnp.int32, v.shape, 1)
    step = 1
    while step < size:
        before = pltpu.roll(v, step, 1)
        after = pltpu.roll(v, count - step, 1)
        v = v + jnp.where((lane & step) != 0, before, after)
        step *= 2
    return v


def moments(parts, held):
    lines = []
    for ref in parts:
        lines += [ref[d] for d in range(ref.shape[0])] if len(ref.shape) == 3 else [ref[...]]
    both = jnp.concatenate(lines, axis=0)
    chans = both.shape[1] // 2
    size = chans // GROUPS
    sums, squares = both[:, :chans], both[:, chans:]
    entries = float(ROWS * held * size)
    total = jnp.broadcast_to(jnp.sum(sums, axis=0, keepdims=True), sums.shape)
    mean = group_sum(total, size) / entries
    off = sums / float(held) - mean
    spread = jnp.sum(squares + float(held) * off * off, axis=0, keepdims=True)
    spread = group_sum(jnp.broadcast_to(spread, sums.shape), size) / entries
    return mean, lax.rsqrt(spread + EPSILON)


def tile_lanes(v, times):
    return jnp.concatenate([v] * times, axis=1) if times > 1 else v


def active(value, mean, gain, shift):
    half = (value.astype(F32) - mean) * gain + shift
    return half + half * jnp.tanh(half)


def piece(block):
    n = block.shape[0]
    origin = jnp.mean(block[0:16], axis=0, keepdims=True)
    d = block - origin
    s = jnp.sum(d, axis=0, keepdims=True)
    q = jnp.sum(d * d, axis=0, keepdims=True)
    return n, s + float(n) * origin, jnp.maximum(q - s * s / float(n), 0.0)


def merge(pieces):
    total = functools.reduce(jnp.add, [s for _, s, _ in pieces])
    mean = total / float(sum(n for n, _, _ in pieces))
    out = functools.reduce(jnp.add, [q for _, _, q in pieces])
    for n, s, _ in pieces:
        off = s / float(n) - mean
        out = out + float(n) * off * off
    return jnp.concatenate([total, out], axis=1)


def publish(ref, vector):
    for d in range(ROWS):
        ref[d] = vector


def next_col(v):
    col = lax.broadcasted_iota(jnp.int32, v.shape, 0) % W
    return jnp.where(col == W - 1, 0.0, pltpu.roll(v, v.shape[0] - 1, 0))


def last_col(v):
    col = lax.broadcasted_iota(jnp.int32, v.shape, 0) % W
    return jnp.where(col == 0, 0.0, pltpu.roll(v, 1, 0))


def edge_flags():
    row = lax.axis_index("rows")
    return row == 0, row == ROWS - 1


def mm(a, b):
    return jnp.dot(a, b, preferred_element_type=F32)


def coarse_stats_kernel(x_ref, out_ref, head_ref, tail_ref):
    x = x_ref[...].astype(F32).reshape(4 * W, 512)
    head_ref[...] = x_ref[0:2]
    tail_ref[...] = x_ref[2:4]
    publish(out_ref, merge([piece(x)]))


def pack_broad(k_ref, out_ref):
    rows = (((0,), (1, 2)), ((0, 1), (2,)))
    step = 128
    for a in range(2):
        for t in range(2):
            for c in range(0, 512, step):
                col = [
                    functools.reduce(
                        jnp.add, [k_ref[ky, kx, c : c + step, :].astype(F32) for ky in rows[a][t]]
                    )
                    for kx in range(3)
                ]
                for n, v in enumerate((col[0], col[1] + col[2], col[0] + col[1], col[2])):
                    out_ref[a, t * 512 + c : t * 512 + c + step, n * 256 : (n + 1) * 256] = v.astype(BF16)


def pack_detail(k_ref, x_ref, z_ref):
    rows = (((0,), (1, 2)), ((0, 1), (2,)))
    for a in range(2):
        for t in range(2):
            col = [
                functools.reduce(jnp.add, [k_ref[ky, kx].astype(F32) for ky in rows[a][t]])
                for kx in range(3)
            ]
            x_ref[a, t] = jnp.concatenate([col[0] + col[1], col[0]], axis=1).astype(BF16)
            z_ref[a, t] = jnp.concatenate([col[2], col[1] + col[2]], axis=1).astype(BF16)


def prepare_kernel_body(
    parts_ref, gain_hbm, shift_hbm, k_hbm, parts_out, gain_ref, shift_ref, w_ref, k_ref, sems
):
    pairs = ((gain_hbm, gain_ref), (shift_hbm, shift_ref)) + tuple((k_hbm.at[i], k_ref.at[i]) for i in range(3))
    copies = [pltpu.make_async_copy(src, dst, sems.at[i]) for i, (src, dst) in enumerate(pairs)]
    for copy in copies:
        copy.start()
    for d in range(ROWS):
        parts_out[d] = parts_ref[d]
    for copy in copies:
        copy.wait()
    pack_broad(k_ref, w_ref)


def broad_entry_kernel_body(
    x_ref, up_ref, down_ref, parts_ref, gain_ref, shift_ref, w_ref, out_ref, stat_ref, an
):
    first, last = edge_flags()
    mean, rate = moments([parts_ref], 4 * W)
    mean, gain, shift = mean[:1], 0.5 * rate[:1] * gain_ref[...], 0.5 * shift_ref[...]
    keep_up = jnp.where(first, 0.0, 1.0)
    keep_down = jnp.where(last, 0.0, 1.0)
    def norm(h):
        if h < 2:
            v = active(up_ref[h], mean, gain, shift) * keep_up
        elif h < 6:
            v = active(x_ref[h - 2], mean, gain, shift)
        else:
            v = active(down_ref[h - 6], mean, gain, shift) * keep_down
        an[h] = v.astype(BF16)

    ready, pieces, count = 0, [], 1
    for start in range(0, 6, count):
        while ready < start + count + 2:
            norm(ready)
            ready += 1
        lo, hi = max(start, 1) - start, min(start + count, 5) - start
        for a in range(2):
            near = an[start + a : start + a + count].reshape(count * W, 512)
            far = an[start + a + 1 : start + a + 1 + count].reshape(count * W, 512)
            both = jnp.concatenate([near, far], axis=1)
            for b in range(2):
                z = mm(both, w_ref[a, :, b * 512 : (b + 1) * 512])
                z = [z[:, 0:256], z[:, 256:512]]
                v = last_col(z[0]) + z[1] if b == 0 else z[0] + next_col(z[1])
                for h in range(count):
                    out_ref[2 * (start + h) + a, :, b * 256 : (b + 1) * 256] = v[h * W : (h + 1) * W].astype(BF16)
                if lo < hi:
                    pieces.append(piece(v[lo * W : hi * W]))
    publish(stat_ref, merge(pieces))


def broad_inner_kernel_body(
    h_ref, x_ref, up_ref, down_ref, parts_ref, gain_ref, shift_ref, w_ref, p_ref,
    out_ref, stat_ref, an,
):
    first, last = edge_flags()
    mean, rate = moments([parts_ref], 8 * 2 * W)
    mean, gain, shift = mean[:1], 0.5 * rate[:1] * gain_ref[...], 0.5 * shift_ref[...]
    mean, gain, shift = (tile_lanes(v, 2) for v in (mean, gain, shift))
    keep_up = jnp.where(first, 0.0, 1.0)
    keep_down = jnp.where(last, 0.0, 1.0)
    def norm(i):
        v = active(h_ref[i], mean, gain, shift)
        if i < 2:
            v = v * keep_up
        elif i >= 10:
            v = v * keep_down
        an[i] = v.astype(BF16)

    skip_in = jnp.concatenate([up_ref[1]] + [x_ref[h] for h in range(4)] + [down_ref[0]], axis=0)
    skip = mm(skip_in, p_ref[...])
    w = w_ref
    even_w = jnp.concatenate([w[ky * 768 + 256 : ky * 768 + 768] for ky in range(3)], axis=0)
    odd_w = jnp.concatenate([w[ky * 768 : ky * 768 + 512] for ky in range(3)], axis=0)
    even_side = jnp.concatenate([w[ky * 768 : ky * 768 + 256] for ky in range(3)], axis=0)
    odd_side = jnp.concatenate([w[ky * 768 + 512 : ky * 768 + 768] for ky in range(3)], axis=0)
    pieces, ready, count = [], 0, 2
    for j in range(0, 10, count):
        while ready < j + count + 2:
            norm(ready)
            ready += 1
        main = jnp.concatenate([an[j + ky : j + ky + count].reshape(count * W, 512) for ky in range(3)], axis=1)
        even_in = jnp.concatenate(
            [an[j + ky : j + ky + count, :, 0:256].reshape(count * W, 256) for ky in range(3)], axis=1
        )
        odd_in = jnp.concatenate(
            [an[j + ky : j + ky + count, :, 256:512].reshape(count * W, 256) for ky in range(3)], axis=1
        )
        extra = jnp.concatenate([skip[(i + 1) // 2 * W : ((i + 1) // 2 + 1) * W] for i in range(j, j + count)], axis=0)
        even = mm(main, even_w) + last_col(mm(odd_in, even_side)) + extra
        odd = mm(main, odd_w) + next_col(mm(even_in, odd_side)) + extra
        for i in range(count):
            out_ref[j + i, :, 0:256] = even[i * W : (i + 1) * W].astype(BF16)
            out_ref[j + i, :, 256:512] = odd[i * W : (i + 1) * W].astype(BF16)
        lo, hi = max(j, 1) - j, min(j + count, 9) - j
        pieces += [piece(v[lo * W : hi * W]) for v in (even, odd)]
    stat_ref[...] = merge(pieces)


def arrange_kernel_body(x_ref, send_hbm, odd_line, even_line, rim, send_ref, sems):
    copies = []

    def ship(at, size):
        rows = pl.ds(at, size)
        copies.append(pltpu.make_async_copy(send_ref.at[:, rows], send_hbm.at[:, rows], sems.at[len(copies)]))
        copies[-1].start()

    even_line[...] = jnp.zeros(even_line.shape, F32)
    rim[...] = jnp.zeros(rim.shape, F32)
    for j in range(10):
        e, o = x_ref[j, :, 0:256].astype(F32), x_ref[j, :, 256:512].astype(F32)
        block = jnp.concatenate([last_col(o).reshape(COLS, 8, 256), e.reshape(COLS, 8, 256)], axis=1)
        send_ref[:, j * 16 : (j + 1) * 16, :] = block.astype(BF16)
        for n in range(2):
            odd_line[j, n] = o[:, n * 128 : (n + 1) * 128]
            even_line[j, n, 0:W] = e[:, n * 128 : (n + 1) * 128]
            rim[n, pl.ds(j, COLS, stride=32), :] = odd_line[j, n, pl.ds(7, COLS, stride=8), :]
            rim[n, pl.ds(10 + j, COLS, stride=32), :] = even_line[j, n, pl.ds(8, COLS, stride=8), :]
        if j in (3, 7):
            ship((j - 3) * 16, 64)
    for n in range(2):
        send_ref[:, 160:192, n * 128 : (n + 1) * 128] = rim[n].reshape(COLS, 32, 128).astype(BF16)
    ship(128, 64)
    for copy in copies:
        copy.wait()


def detail_stats_kernel_body(
    x_ref, a_ref, b_ref, c_ref, d_ref, gain_ref, shift_ref, k_ref, stat_ref, norm_ref, an, wx_ref, wz_ref
):
    pack_detail(k_ref, wx_ref, wz_ref)
    first, last = edge_flags()
    mean, rate = moments([a_ref, b_ref, c_ref, d_ref], 8 * 2 * W)
    norm_ref[...] = jnp.concatenate([mean[:1], rate[:1]], axis=1)
    mean, gain, shift = mean[:1], 0.5 * rate[:1] * gain_ref[...], 0.5 * shift_ref[...]
    mean, gain, shift = (tile_lanes(v, 2) for v in (mean, gain, shift))
    keep_up = jnp.where(first, 0.0, 1.0)
    keep_down = jnp.where(last, 0.0, 1.0)
    def norm(i):
        v = active(x_ref[i], mean, gain, shift)
        if i < 1:
            v = v * keep_up
        elif i >= 9:
            v = v * keep_down
        an[i] = v.astype(BF16)

    pieces, ready, count = [], 0, 4
    for start in range(0, 9 - count, count):
        while ready < start + count + 2:
            norm(ready)
            ready += 1
        for a in range(2):
            lhs = [an[start + a + t : start + a + t + count].reshape(count * W, 512) for t in range(2)]
            main = jnp.concatenate(lhs, axis=1)
            odd = jnp.concatenate([v[:, 256:512] for v in lhs], axis=1)
            even = jnp.concatenate([v[:, 0:256] for v in lhs], axis=1)
            wx = [wx_ref[a, t] for t in range(2)]
            wz = [wz_ref[a, t] for t in range(2)]
            middle = mm(main, jnp.concatenate([wx[0], wz[0], wx[1], wz[1]], axis=0))
            right = mm(odd, jnp.concatenate(wx, axis=0))
            left = mm(even, jnp.concatenate(wz, axis=0))
            q3 = right[:, 0:128] + next_col(left[:, 0:128])
            q0 = last_col(right[:, 128:256]) + left[:, 128:256]
            pieces += [piece(v) for v in (q3, q0, middle[:, 0:128], middle[:, 128:256])]
    stat_ref[...] = merge(pieces)


def summary_kernel_body(here_ref, there_ref, norm_ref, out_ref):
    mean, rate = moments([here_ref, there_ref], 16 * 4 * W)
    both = jnp.concatenate([mean[:1], rate[:1], norm_ref[...]], axis=1)
    for c in range(COLS):
        out_ref[c] = both


def pixel(j, u):
    if u == 15:
        return 160 + j
    if u == 16:
        return 170 + j
    return j * 16 + (8 + u // 2 if u % 2 == 0 else (u + 1) // 2)


PLAN = (('entry', 0, 3), ('entry', 3, 3), ('entry', 6, 3), ('inner', 0, 4), ('inner', 4, 4), ('send', 0, 8), ('inner', 8, 4), ('inner', 12, 4), ('send', 8, 8))


def detail_kernel_body(
    x_ref, norm_ref, gain3_ref, shift3_ref, gain4_ref, shift4_ref, k3_ref, k4_ref, p_ref,
    out_hbm, an3, an4, wx_ref, wz_ref, w_ref, tmp, out_ref, sems,
):
    pack_detail(k3_ref, wx_ref, wz_ref)
    zero = jnp.zeros((128, 128), BF16)
    for ky in range(3):
        k = [k4_ref[ky, kx] for kx in range(3)]
        table = ((k[0], zero), (k[1], k[0]), (k[2], k[1]), (zero, k[2]))
        for i, pair in enumerate(table):
            at = ky * 512 + i * 128
            w_ref[at : at + 128, 0:128] = pair[0]
            w_ref[at : at + 128, 128:256] = pair[1]
    first, last = edge_flags()
    keep_up = jnp.where(first, 0.0, 1.0)
    keep_down = jnp.where(last, 0.0, 1.0)
    col = lax.axis_index("cols")
    keep_left = jnp.where(col == 0, 0.0, 1.0)
    keep_right = jnp.where(col == COLS - 1, 0.0, 1.0)
    norm = jnp.concatenate([norm_ref[i] for i in range(COLS)], axis=0)
    mean4, rate4 = (tile_lanes(norm[:, n * 128 : (n + 1) * 128], 2) for n in range(2))
    mean3, rate3 = norm[:, 256:512], norm[:, 512:768]
    gain3, shift3 = 0.5 * rate3 * gain3_ref[...], 0.5 * shift3_ref[...]
    gain4, shift4 = 0.5 * rate4 * tile_lanes(gain4_ref[...], 2), 0.5 * tile_lanes(shift4_ref[...], 2)
    def norm3(j):
        for u in range(-1, 17):
            v = active(x_ref[pixel(j, u)], mean3, gain3, shift3)
            if j == 0:
                v = v * keep_up
            elif j == 9:
                v = v * keep_down
            if u == -1:
                v = v * keep_left
            elif u == 16:
                v = v * keep_right
            an3[j, (u + 1) * 16 : (u + 2) * 16] = v.astype(BF16)

    size = 17 * 16
    lane = lax.broadcasted_iota(jnp.int32, (16, 256), 1)
    left_mask = jnp.where(lane < 128, keep_left, 1.0)
    right_mask = jnp.where(lane >= 128, keep_right, 1.0)

    def entry(i, count):
        lhs = jnp.concatenate(
            [
                an3[i + t : i + t + count, s : s + size].reshape(count * size, 256)
                for t in range(2)
                for s in (0, 16)
            ],
            axis=1,
        )
        w = [jnp.concatenate([wx_ref[a, 0], wz_ref[a, 0], wx_ref[a, 1], wz_ref[a, 1]], axis=0) for a in range(2)]
        both = mm(lhs, jnp.concatenate(w, axis=1))
        for a in range(2):
            v = both[:, a * 256 : (a + 1) * 256].astype(BF16).reshape(count * 17, 16, 256)
            v = active(v, mean4, gain4, shift4)
            for n in range(count):
                f = 2 * (i + n) + 1 - a
                line = v[n * 17 : (n + 1) * 17]
                if f == 0:
                    line = line * keep_up
                elif f == 17:
                    line = line * keep_down
                an4[f, 16 : size - 16] = line[1:16].reshape(15 * 16, 256).astype(BF16)
                an4[f, 0:16] = (line[0] * left_mask).astype(BF16)
                an4[f, size - 16 : size] = (line[16] * right_mask).astype(BF16)

    def inner(base, count):
        lhs = jnp.concatenate(
            [an4[base + ky : base + ky + count, s : s + 256].reshape(count * 256, 256) for ky in range(3) for s in (0, 16)],
            axis=1,
        )
        v = mm(lhs, w_ref[...])
        raw = [x_ref[pixel(j, u)] for j in range(base // 2 + 1, (base + count) // 2 + 1) for u in range(16)]
        skip = mm(jnp.concatenate(raw, axis=0), p_ref[...])
        for n in range(count):
            for b in range(2):
                part = v[n * 256 : (n + 1) * 256, b * 128 : (b + 1) * 128] + skip[n // 2 * 256 : (n // 2 + 1) * 256]
                for u in range(16):
                    at = (2 * u + b) * 16
                    tmp[n, at : at + 16] = part[u * 16 : (u + 1) * 16]
            for image in range(16):
                out_ref[image, base + n] = tmp[n, pl.ds(image, 32, stride=16), :].astype(BF16)

    copies = []

    def send(base, count):
        rows = pl.ds(base, count)
        copies.append(pltpu.make_async_copy(out_ref.at[:, rows], out_hbm.at[:, rows], sems.at[len(copies)]))
        copies[-1].start()

    ready = 0
    for kind, base, count in PLAN:
        if kind == "entry":
            while ready < base + count + 1:
                norm3(ready)
                ready += 1
            entry(base, count)
        elif kind == "inner":
            inner(base, count)
        else:
            send(base, count)
    for copy in copies:
        copy.wait()


def swap(parts):
    return lax.all_to_all(parts, "rows", 0, 0, tiled=True)


def across_z(v):
    return lax.ppermute(v, "rows", [(i, i ^ 1) for i in range(ROWS)])


def along_y(v):
    return [lax.ppermute(v, "rows", [(i, (i + 2 * k) % ROWS) for i in range(ROWS)]) for k in range(1, 4)]


def shape(*dims, dtype=BF16):
    return jax.ShapeDtypeStruct(dims, dtype)


def stay(v):
    return pltpu.with_memory_space_constraint(v, pltpu.HBM)


def line(v):
    return v.reshape(1, -1)


def detail_call(*operands):
    return pl.pallas_call(
        detail_kernel_body,
        in_specs=[VMEM] * len(operands),
        out_specs=HBM,
        out_shape=shape(COLS, 16, 32, 128),
        scratch_shapes=[
            pltpu.VMEM((10, 18 * 16, 256), BF16),
            pltpu.VMEM((18, 17 * 16, 256), BF16),
            pltpu.VMEM((2, 2, 256, 256), BF16),
            pltpu.VMEM((2, 2, 256, 256), BF16),
            pltpu.VMEM((1536, 256), BF16),
            pltpu.VMEM((8, 512, 128), F32),
            pltpu.VMEM((COLS, 16, 32, 128), BF16),
            pltpu.SemaphoreType.DMA((6,)),
        ],
        name="detail",
        cost_estimate=pl.CostEstimate(flops=1 << 33, bytes_accessed=0, transcendentals=0),
        compiler_params=pltpu.CompilerParams(vmem_limit_bytes=VMEM_LIMIT),
    )(*operands)


def body(
    coarse,
    broad_entry_scale,
    broad_entry_bias,
    broad_entry_kernel,
    broad_inner_scale,
    broad_inner_bias,
    broad_inner_kernel,
    broad_skip_projection,
    detail_entry_scale,
    detail_entry_bias,
    detail_entry_kernel,
    detail_inner_scale,
    detail_inner_bias,
    detail_inner_kernel,
    detail_skip_projection,
):
    x = coarse.reshape(4, W, 512)
    stat = lambda c: shape(ROWS, 1, 2 * c, dtype=F32)
    parts, head, tail = call(
        coarse_stats_kernel, (stat(512), shape(2, W, 512), shape(2, W, 512)), name="coarse_stats"
    )(x)
    up = lax.ppermute(tail, "rows", [(i, (i + 1) % ROWS) for i in range(ROWS)])
    down = lax.ppermute(head, "rows", [((i + 1) % ROWS, i) for i in range(ROWS)])
    parts, gain, shift, packed = call(
        prepare_kernel_body,
        (stat(512), shape(1, 512, dtype=F32), shape(1, 512, dtype=F32), shape(2, 1024, 1024)),
        [pltpu.VMEM((3, 3, 512, 256), BF16), pltpu.SemaphoreType.DMA((5,))],
        name="prepare",
        flops=1 << 30,
        specs=[VMEM] + [HBM] * 3,
    )(parts, *(stay(v) for v in (line(broad_entry_scale), line(broad_entry_bias), broad_entry_kernel)))
    parts = swap(parts)
    wide_h, parts = call(
        broad_entry_kernel_body,
        (shape(12, W, 512), stat(256)),
        [pltpu.VMEM((8, W, 512), BF16)],
        name="broad_entry",
        flops=1 << 32,
    )(x, up, down, parts, gain, shift, packed)
    parts = swap(parts)
    wide_out, part = call(
        broad_inner_kernel_body,
        (shape(10, W, 512), shape(1, 512, dtype=F32)),
        [pltpu.VMEM((12, W, 512), BF16)],
        name="broad_inner",
        flops=1 << 32,
    )(
        wide_h,
        x,
        up,
        down,
        parts,
        line(broad_inner_scale),
        line(broad_inner_bias),
        broad_inner_kernel.reshape(9 * 256, 256),
        broad_skip_projection,
    )
    send = call(
        arrange_kernel_body,
        shape(COLS, 192, 256),
        [
            pltpu.VMEM((10, 2, W, 128), F32),
            pltpu.VMEM((10, 2, W + 8, 128), F32),
            pltpu.VMEM((2, COLS * 32, 128), F32),
            pltpu.VMEM((COLS, 192, 256), BF16),
            pltpu.SemaphoreType.DMA((3,)),
        ],
        name="arrange",
        flops=1 << 30,
        outs=HBM,
    )(wide_out)
    pair = jnp.concatenate([part, across_z(part)], axis=0)
    send, pair = lax.optimization_barrier((send, pair))
    blocks = lax.all_to_all(send, "cols", 0, 0, tiled=True)
    part, norm = call(
        detail_stats_kernel_body,
        (shape(1, 256, dtype=F32), shape(1, 512, dtype=F32)),
        [pltpu.VMEM((10, W, 512), BF16)] + [pltpu.VMEM((2, 2, 256, 256), BF16)] * 2,
        name="detail_stats",
        flops=1 << 32,
    )(wide_out, pair, *along_y(pair), line(detail_entry_scale), line(detail_entry_bias), detail_entry_kernel)
    here = jnp.concatenate([part] + along_y(part), axis=0)
    there = across_z(here)
    norms = call(summary_kernel_body, shape(COLS, 1, 768, dtype=F32), name="summary")(here, there, norm)
    blocks, norms = lax.optimization_barrier((blocks, norms))
    norms = lax.all_to_all(norms, "cols", 0, 0, tiled=True)
    blocks = jnp.transpose(blocks, (1, 0, 2))
    return detail_call(
        blocks,
        norms,
        line(detail_entry_scale),
        line(detail_entry_bias),
        line(detail_inner_scale),
        line(detail_inner_bias),
        detail_entry_kernel,
        detail_inner_kernel,
        detail_skip_projection,
    )


def solution(mesh):
    return jax.shard_map(
        body,
        mesh=mesh,
        in_specs=(P("cols", "rows", None, None),) + (P(),) * 14,
        out_specs=P(None, "rows", "cols", None),
        check_vma=False,
    )
```
